32 devices in a mesh: seq: 2 (over core), heads: 4 (over y, x), dp: 4 (over z).
Axes of the slice: x: 2, y: 2, z: 4, core: 2. Of those that a mesh axis runs over, the one named last changes fastest.
Arguments:
- tokens: bfloat16 [4, 256, 3072], P('dp', 'seq'), may hold values from -6 to 6
- proj_weights: bfloat16 [3, 3072, 4096], P(None, 'seq', ('heads', 'dp')), may hold values from -0.109375 to 0.109375
- norm_gain: float32 [4096], P(('heads', 'dp')), may hold values from 0.5 to 1.5
Outputs:
- attended: bfloat16 [4, 256, 4096], P('dp', 'seq', 'heads')
The draws below stay inside these ranges and needn't reach their ends.
All inputs are finite; a program needn't handle non-finite values.
Results may differ from the reference program's by a relative error of at most 0.0063.
Values may be sent and summed in bfloat16 or wider, within the bound.
A program may use at most 64 MiB of HBM per device.

```python
import jax
import jax.numpy as jnp
from jax import lax

D = 3072
HEADS = 32
DH = 128
TOK_DEV = 128
SEQS = 4
LENGTH = 256
N_SEQ = 2


def level_of(rng, extent, shards, smallest, top_value):
    def one(dim, blocks):
        draws = jax.random.uniform(jax.random.fold_in(jax.random.fold_in(rng, 6), dim), (blocks,), jnp.float32, smallest / len(shards), top_value / len(shards))
        return jnp.repeat(jnp.exp(draws), extent[dim] // blocks).reshape((-1,) + (1,) * (len(extent) - dim - 1))

    level = one(*shards[0])
    for cut in shards[1:]:
        level = level * one(*cut)
    return level


def scatter_about(own_key, extent, width, limit, split=(), kind=jnp.bfloat16):
    drawn = jax.random.normal(own_key, extent, jnp.float32) * width
    if len(split) > 0:
        drawn = level_of(own_key, extent, split, -0.22, 0.18) * drawn
    return jnp.clip(drawn, min=-limit, max=limit).astype(kind)


def setup_inputs(seed: int = 0) -> dict:
    arg_keys = jax.random.split(jax.random.key(seed), 4)
    tokens = scatter_about(arg_keys[0], (SEQS, LENGTH, D), 1.0, 6.0, ((0, 4), (1, 2)))
    proj_weights = scatter_about(arg_keys[1], (3, D, HEADS * DH), D ** -0.5, 0.109375, ((1, 2), (2, 16)))
    norm_gain = jnp.clip(1.0 + 0.1 * jax.random.normal(arg_keys[2], (HEADS * DH,), jnp.float32), 0.5, 1.5)
    return {"tokens": tokens, "proj_weights": proj_weights, "norm_gain": norm_gain}


def one_sequence(rows, proj_weights, norm_gain):
    blocks = N_SEQ
    queries = jax.nn.silu(jnp.dot(rows, proj_weights[0], preferred_element_type=jnp.float32)).astype(jnp.bfloat16)
    keys = jax.nn.silu(jnp.dot(rows, proj_weights[1], preferred_element_type=jnp.float32)).astype(jnp.bfloat16)
    values = jnp.dot(rows, proj_weights[2], preferred_element_type=jnp.float32).astype(jnp.bfloat16)
    query_f = queries.astype(jnp.float32).reshape(blocks, TOK_DEV, HEADS, DH)
    key_f = keys.astype(jnp.float32).reshape(blocks, TOK_DEV, HEADS, DH)
    value_f = values.astype(jnp.float32).reshape(blocks, TOK_DEV, HEADS, DH)
    state = jnp.einsum('nthd,nthe->nhde', key_f, value_f)
    running = jnp.cumsum(state, axis=0)
    prefix = jnp.concatenate([jnp.zeros((1, HEADS, DH, DH), jnp.float32), running[:-1]], axis=0)
    prefix_b = prefix.astype(jnp.bfloat16).astype(jnp.float32)
    scores = jnp.einsum('nthd,nuhd->nhtu', query_f, key_f)
    causal = lax.broadcasted_iota(jnp.int32, (TOK_DEV, TOK_DEV), 0) >= lax.broadcasted_iota(jnp.int32, (TOK_DEV, TOK_DEV), 1)
    scores_b = jnp.where(causal, scores, 0.0).astype(jnp.bfloat16).astype(jnp.float32)
    local = jnp.einsum('nhtu,nuhd->nthd', scores_b, value_f)
    carried = jnp.einsum('nthd,nhde->nthe', query_f, prefix_b)
    attn = local + carried
    scale = lax.rsqrt(lax.optimization_barrier(jnp.mean(attn * attn, axis=-1, keepdims=True)) + 1e-06)
    normed = attn * scale * norm_gain.reshape(HEADS, DH)
    return normed.reshape(LENGTH, HEADS * DH).astype(jnp.bfloat16)

def reference(tokens, proj_weights, norm_gain):
    results = [one_sequence(tokens[index], proj_weights, norm_gain) for index in range(SEQS)]
    return jnp.stack(results, axis=0)
```

```python
import functools

import jax
import jax.numpy as jnp
from jax import lax
from jax.experimental import pallas as pl
from jax.experimental.pallas import tpu as pltpu
from jax.sharding import PartitionSpec as P

DH = 128
SUBS = 3
TURNS = SUBS + 1
MESH = pl.DeviceIdType.MESH


def kernel(
    sizes, tokens, weights, gain, out,
    tok, own, w, acc, queries, stage, state_out, state_in,
    own_sem, w_sem, w_send, w_recv, up_send, down_send, z_recv,
    x_send, x_recv, y_send, y_recv, st_send, st_recv, o_send, o_recv, o_sem,
):
    n_seq, n_heads, n_dp = sizes
    c, h, d = lax.axis_index("seq"), lax.axis_index("heads"), lax.axis_index("dp")
    length = own.shape[0]
    rows, cols = weights.shape[1], weights.shape[2]
    block = tok.shape[3]
    heads = cols // DH
    xp = h + 1 - 2 * (h % 2)
    yp = h + 2 - 4 * (h // 2)
    across = xp + yp - h

    def remote(src, dst, send, recv, **device):
        return pltpu.make_async_remote_copy(
            src_ref=src, dst_ref=dst, send_sem=send, recv_sem=recv,
            device_id=device, device_id_type=MESH,
        )

    own_copy = pltpu.make_async_copy(tokens.at[0], own, own_sem)
    own_copy.start()
    my_rows = w.at[:, pl.ds(pl.multiple_of(c * rows, 16), rows), :]
    w_copy = pltpu.make_async_copy(weights, my_rows, w_sem)
    w_copy.start()

    barrier = pltpu.get_barrier_semaphore()
    for o in range(1, n_dp):
        pl.semaphore_signal(barrier, inc=1, device_id={"dp": (d + o) % n_dp}, device_id_type=MESH)
    for o in range(1, n_seq):
        pl.semaphore_signal(barrier, inc=1, device_id={"seq": (c + o) % n_seq}, device_id_type=MESH)
    pl.semaphore_signal(barrier, inc=1, device_id={"heads": xp}, device_id_type=MESH)
    pl.semaphore_signal(barrier, inc=1, device_id={"heads": yp}, device_id_type=MESH)
    pl.semaphore_wait(barrier, n_dp + n_seq)

    def z_block(i):
        last = i // SUBS
        return (1 - last) * (h * SUBS + SUBS - 1 - i) + last * across * SUBS

    def x_block(i):
        last = i // SUBS
        return (1 - last) * (xp * SUBS + SUBS - 1 - i) + last * (across * SUBS + 1)

    def y_block(i):
        last = i // SUBS
        return (1 - last) * (yp * SUBS + SUBS - 1 - i) + last * (across * SUBS + 2)

    def first(i, up):
        b = z_block(i)
        src = tokens.at[0, :, pl.ds(pl.multiple_of(b * block, block), block)]
        return remote(
            src, tok.at[d, b], (up_send if up else down_send).at[d, i], z_recv.at[d, i],
            dp=d + 1 if up else d - 1,
        )

    def along(s, i, up):
        b = z_block(i)
        return remote(
            tok.at[s, b], tok.at[s, b], (up_send if up else down_send).at[s, i],
            z_recv.at[s, i], dp=d + 1 if up else d - 1,
        )

    def to_x(s, i, b):
        return remote(tok.at[s, b], tok.at[s, b], x_send.at[s, i], x_recv.at[s, i], heads=xp)

    def to_y(s, i, b):
        return remote(tok.at[s, b], tok.at[s, b], y_send.at[s, i], y_recv.at[s, i], heads=yp)

    for i in range(TURNS):
        @pl.when(d < n_dp - 1)
        def _():
            first(i, True).start()

        @pl.when(d > 0)
        def _():
            first(i, False).start()

    def share(o):
        return remote(
            weights, my_rows, w_send.at[o - 1], w_recv.at[o - 1], seq=(c + o) % n_seq
        )

    for o in range(1, n_seq):
        share(o).start()

    def for_sources(k, do):
        @pl.when(d - k >= 0)
        def _():
            do(d - k, True)

        @pl.when(d + k < n_dp)
        def _():
            do(d + k, False)

    def z_phase(t):
        i = t % TURNS

        def one(s, up):
            b = z_block(i)
            along(s, i, up).wait_recv()
            @pl.when(d < n_dp - 1 if up else d > 0)
            def _():
                along(s, i, up).start()

            @pl.when(i < SUBS)
            def _():
                to_x(s, i, b).start()
                to_y(s, i, b).start()

        for_sources(t // TURNS + 1, one)

    def xy_phase(t):
        i = t % TURNS

        def one(s, up):
            to_x(s, i, x_block(i)).wait_recv()

            @pl.when(i == 0)
            def _():
                to_y(s, SUBS, x_block(0)).start()

            to_y(s, i, y_block(i)).wait_recv()

            @pl.when(i == 1)
            def _():
                to_x(s, SUBS, y_block(1)).start()

        for_sources(t // TURNS + 1, one)

    def times(piece, b):
        k_rows = pl.ds(pl.multiple_of(b * block, block), block)
        return [
            jnp.dot(piece, w[j, k_rows, :], preferred_element_type=jnp.float32)
            for j in range(3)
        ]

    def add(s, i, parts):
        for j in range(3):
            new = parts[0][j] + parts[1][j] + parts[2][j]
            @pl.when(i == 0)
            def _():
                acc[s, j] = new

            @pl.when(i > 0)
            def _():
                acc[s, j] += new

    def state_to(s, o):
        return remote(
            state_out.at[s], state_in.at[o - 1, s], st_send.at[o - 1, s], st_recv.at[o - 1, s],
            seq=(c + o) % n_seq,
        )

    def silu(v):
        return v / (1.0 + jnp.exp(-v))

    def finish_local(s):
        causal = lax.broadcasted_iota(jnp.int32, (length, length), 0) >= lax.broadcasted_iota(
            jnp.int32, (length, length), 1
        )
        kept = []
        for head in range(heads):
            at = slice(head * DH, (head + 1) * DH)
            k = silu(acc[s, 1, :, at]).astype(jnp.bfloat16)
            v = acc[s, 2, :, at].astype(jnp.bfloat16)
            state = lax.dot_general(k, v, (((0,), (0,)), ((), ())), preferred_element_type=jnp.float32)
            state_out[s, head] = state.astype(jnp.bfloat16)
            kept.append((k, v))

        @pl.loop(1, n_seq - c)
        def _(o):
            state_to(s, o).start()

        for head in range(heads):
            at = slice(head * DH, (head + 1) * DH)
            k, v = kept[head]
            q = silu(acc[s, 0, :, at]).astype(jnp.bfloat16)
            scores = lax.dot_general(q, k, (((1,), (1,)), ((), ())), preferred_element_type=jnp.float32)
            scores_b = jnp.where(causal, scores, 0.0).astype(jnp.bfloat16)
            queries[s, :, at] = q
            acc[s, 0, :, at] = jnp.dot(scores_b, v, preferred_element_type=jnp.float32)

    def to_owner(s):
        at = pl.ds(pl.multiple_of(d * cols, cols), cols)
        return remote(stage.at[s], out.at[0, :, at], o_send.at[s], o_recv.at[d], dp=s)

    def keep(s):
        at = pl.ds(pl.multiple_of(d * cols, cols), cols)
        return pltpu.make_async_copy(stage.at[s], out.at[0, :, at], o_sem)

    def finish_carried(s):
        @pl.when(c > 0)
        def _():
            @pl.loop(1, c + 1)
            def _(o):
                state_to(s, o).wait_recv()

            for head in range(heads):
                at = slice(head * DH, (head + 1) * DH)
                prefix = lax.fori_loop(
                    1, c + 1,
                    lambda o, total: total + state_in[o - 1, s, head].astype(jnp.float32),
                    jnp.zeros((DH, DH), jnp.float32),
                )
                acc[s, 0, :, at] += jnp.dot(
                    queries[s, :, at], prefix.astype(jnp.bfloat16),
                    preferred_element_type=jnp.float32,
                )

        for head in range(heads):
            at = slice(head * DH, (head + 1) * DH)
            attn = acc[s, 0, :, at]
            scale = lax.rsqrt(jnp.mean(attn * attn, axis=-1, keepdims=True) + 1e-06)
            stage[s, :, at] = (attn * scale * gain[:, at]).astype(jnp.bfloat16)

    def compute(t):
        i = t % TURNS

        @pl.when(t < TURNS)
        def _():
            parts = []
            for n in range(SUBS):
                b = t * SUBS + n
                piece = own[:, pl.ds(pl.multiple_of(b * block, block), block)]
                parts.append(times(piece, b))
            add(d, i, parts)

            @pl.when(i == TURNS - 1)
            def _():
                finish_local(d)

        def one(s, up):
            blocks = (z_block(i), x_block(i), y_block(i))
            add(s, i, [times(tok[s, b], b) for b in blocks])

            @pl.when(i == TURNS - 1)
            def _():
                finish_local(s)

        for_sources(t // TURNS + 1, one)

    def output(t):
        @pl.when(t % TURNS == TURNS - 1)
        def _():
            @pl.when(t < TURNS)
            def _():
                finish_carried(d)
                keep(d).start()

            def one(s, up):
                finish_carried(s)
                to_owner(s).start()

            for_sources(t // TURNS + 1, one)

    turns = (n_dp - 1) * TURNS
    z_phase(0)
    z_phase(1)
    xy_phase(0)
    own_copy.wait()
    w_copy.wait()
    for o in range(1, n_seq):
        share(o).wait_recv()
    compute(0)

    @pl.loop(2, turns + 2)
    def _(t):
        @pl.when(t < turns)
        def _():
            z_phase(t)

        @pl.when(t <= turns)
        def _():
            xy_phase(t - 1)
            compute(t - 1)

        output(t - 2)

    for o in range(1, n_seq):
        share(o).wait_send()

    for i in range(TURNS):
        @pl.when(d < n_dp - 1)
        def _():
            first(i, True).wait_send()

        @pl.when(d > 0)
        def _():
            first(i, False).wait_send()

    @pl.loop(0, turns)
    def _(t):
        i = t % TURNS

        def one(s, up):
            @pl.when(d < n_dp - 1 if up else d > 0)
            def _():
                along(s, i, up).wait_send()

            to_x(s, i, z_block(i)).wait_send()
            to_y(s, i, z_block(i)).wait_send()

        for_sources(t // TURNS + 1, one)

    @pl.loop(0, n_dp)
    def _(s):
        @pl.loop(1, n_seq - c)
        def _(o):
            state_to(s, o).wait_send()

        @pl.when(s != d)
        def _():
            to_owner(s).wait_send()
            at = pl.ds(pl.multiple_of(s * cols, cols), cols)
            remote(stage.at[s], out.at[0, :, at], o_send.at[s], o_recv.at[s], dp=s).wait_recv()

    keep(d).wait()


def body(sizes, tokens, proj_weights, norm_gain):
    n_seq, n_heads, n_dp = sizes
    _, length, width = tokens.shape
    _, rows, cols = proj_weights.shape
    pieces = n_heads * SUBS
    block = width // pieces
    heads = cols // DH
    dma = pltpu.SemaphoreType.DMA
    any_space = pl.BlockSpec(memory_space=pl.ANY)
    flops = 2 * n_dp * length * width * 3 * cols
    return pl.pallas_call(
        functools.partial(kernel, sizes),
        out_shape=jax.ShapeDtypeStruct((1, length, n_dp * cols), jnp.bfloat16),
        in_specs=[any_space, any_space, pl.BlockSpec(memory_space=pltpu.VMEM)],
        out_specs=any_space,
        scratch_shapes=[
            pltpu.VMEM((n_dp, pieces, length, block), jnp.bfloat16),
            pltpu.VMEM((length, width), jnp.bfloat16),
            pltpu.VMEM((3, width, cols), jnp.bfloat16),
            pltpu.VMEM((n_dp, 3, length, cols), jnp.float32),
            pltpu.VMEM((n_dp, length, cols), jnp.bfloat16),
            pltpu.VMEM((n_dp, length, cols), jnp.bfloat16),
            pltpu.VMEM((n_dp, heads, DH, DH), jnp.bfloat16),
            pltpu.VMEM((n_seq - 1, n_dp, heads, DH, DH), jnp.bfloat16),
            dma, dma, dma((n_seq - 1,)), dma((n_seq - 1,)),
            dma((n_dp, TURNS)), dma((n_dp, TURNS)), dma((n_dp, TURNS)),
            dma((n_dp, TURNS)), dma((n_dp, TURNS)), dma((n_dp, TURNS)), dma((n_dp, TURNS)),
            dma((n_seq - 1, n_dp)), dma((n_seq - 1, n_dp)),
            dma((n_dp,)), dma((n_dp,)), dma,
        ],
        compiler_params=pltpu.CompilerParams(
            collective_id=0, has_side_effects=True, vmem_limit_bytes=48 * 1024 * 1024
        ),
        cost_estimate=pl.CostEstimate(
            flops=flops, bytes_accessed=2 * (tokens.size + proj_weights.size), transcendentals=0
        ),
    )(tokens, proj_weights, norm_gain.reshape(1, cols))


def solution(mesh):
    sizes = tuple(mesh.shape[name] for name in ("seq", "heads", "dp"))
    in_specs = (P("dp", "seq", None), P(None, "seq", ("heads", "dp")), P(("heads", "dp")))
    out_specs = P("dp", "seq", "heads")
    return jax.shard_map(
        functools.partial(body, sizes), mesh=mesh, in_specs=in_specs, out_specs=out_specs, check_vma=False
    )
```

```python
import functools

import jax
import jax.numpy as jnp
from jax import lax
from jax.experimental import pallas as pl
from jax.experimental.pallas import tpu as pltpu
from jax.sharding import PartitionSpec as P

DH = 128
SUBS = 3
TURNS = SUBS + 1
LAG = 2
START = 5
EVEN = 2 * START - LAG
OWN_AT = 1
MESH = pl.DeviceIdType.MESH


def kernel(
    sizes, tokens, weights, gain, out,
    tok, own, w, acc, queries, stage, state_out, state_in,
    own_sem, w_sem, w_send, w_recv, up_send, down_send, z_recv,
    x_send, x_recv, y_send, y_recv, st_send, st_recv, o_send, o_recv, o_sem,
):
    n_seq, n_heads, n_dp = sizes
    c, h, d = lax.axis_index("seq"), lax.axis_index("heads"), lax.axis_index("dp")
    length = own.shape[0]
    rows, cols = weights.shape[1], weights.shape[2]
    block = tok.shape[3]
    heads = cols // DH
    xp = h + 1 - 2 * (h % 2)
    yp = h + 2 - 4 * (h // 2)
    across = xp + yp - h

    def remote(src, dst, send, recv, **device):
        return pltpu.make_async_remote_copy(
            src_ref=src, dst_ref=dst, send_sem=send, recv_sem=recv,
            device_id=device, device_id_type=MESH,
        )

    own_copy = pltpu.make_async_copy(tokens.at[0], own, own_sem)
    own_copy.start()
    my_rows = w.at[:, pl.ds(pl.multiple_of(c * rows, 16), rows), :]
    w_copy = pltpu.make_async_copy(weights, my_rows, w_sem)
    w_copy.start()

    barrier = pltpu.get_barrier_semaphore()
    for o in range(1, n_dp):
        pl.semaphore_signal(barrier, inc=1, device_id={"dp": (d + o) % n_dp}, device_id_type=MESH)
    for o in range(1, n_seq):
        pl.semaphore_signal(barrier, inc=1, device_id={"seq": (c + o) % n_seq}, device_id_type=MESH)
    pl.semaphore_signal(barrier, inc=1, device_id={"heads": xp}, device_id_type=MESH)
    pl.semaphore_signal(barrier, inc=1, device_id={"heads": yp}, device_id_type=MESH)
    pl.semaphore_wait(barrier, n_dp + n_seq)

    def z_block(i):
        last = i // SUBS
        return (1 - last) * (h * SUBS + SUBS - 1 - i) + last * across * SUBS

    def x_block(i):
        last = i // SUBS
        return (1 - last) * (xp * SUBS + SUBS - 1 - i) + last * (across * SUBS + 1)

    def y_block(i):
        last = i // SUBS
        return (1 - last) * (yp * SUBS + SUBS - 1 - i) + last * (across * SUBS + 2)

    def first(i, up):
        b = z_block(i)
        src = tokens.at[0, :, pl.ds(pl.multiple_of(b * block, block), block)]
        return remote(
            src, tok.at[d, b], (up_send if up else down_send).at[d, i], z_recv.at[d, i],
            dp=d + 1 if up else d - 1,
        )

    def along(s, i, up):
        b = z_block(i)
        return remote(
            tok.at[s, b], tok.at[s, b], (up_send if up else down_send).at[s, i],
            z_recv.at[s, i], dp=d + 1 if up else d - 1,
        )

    def to_x(s, i, b):
        return remote(tok.at[s, b], tok.at[s, b], x_send.at[s, i], x_recv.at[s, i], heads=xp)

    def to_y(s, i, b):
        return remote(tok.at[s, b], tok.at[s, b], y_send.at[s, i], y_recv.at[s, i], heads=yp)

    for i in range(TURNS):
        @pl.when(d < n_dp - 1)
        def _():
            first(i, True).start()

        @pl.when(d > 0)
        def _():
            first(i, False).start()

    def share(o, j):
        return remote(
            weights.at[j], my_rows.at[j], w_send.at[o - 1, j], w_recv.at[o - 1, j],
            seq=(c + o) % n_seq,
        )

    for o in range(1, n_seq):
        for j in range(3):
            share(o, j).start()

    acc[...] = jnp.zeros_like(acc)

    def for_sources(k, do):
        @pl.when(d - k >= 0)
        def _():
            do(d - k, True)

        @pl.when(d + k < n_dp)
        def _():
            do(d + k, False)

    def z_phase(t):
        i = t % TURNS

        def one(s, up):
            b = z_block(i)
            along(s, i, up).wait_recv()
            @pl.when(d < n_dp - 1 if up else d > 0)
            def _():
                along(s, i, up).start()

            @pl.when(i < SUBS)
            def _():
                to_x(s, i, b).start()
                to_y(s, i, b).start()

        for_sources(t // TURNS + 1, one)

    def xy_phase(t):
        i = t % TURNS

        def one(s, up):
            to_x(s, i, x_block(i)).wait_recv()

            @pl.when(i == 0)
            def _():
                to_y(s, SUBS, x_block(0)).start()

            to_y(s, i, y_block(i)).wait_recv()

            @pl.when(i == 1)
            def _():
                to_x(s, SUBS, y_block(1)).start()

        for_sources(t // TURNS + 1, one)

    def times(piece, b):
        k_rows = pl.ds(pl.multiple_of(b * block, block), block)
        return [
            jnp.dot(piece, w[j, k_rows, :], preferred_element_type=jnp.float32)
            for j in range(3)
        ]

    def add(s, parts):
        for j in range(3):
            acc[s, j] += parts[0][j] + parts[1][j] + parts[2][j]

    def state_to(s, o):
        return remote(
            state_out.at[s], state_in.at[o - 1, s], st_send.at[o - 1, s], st_recv.at[o - 1, s],
            seq=(c + o) % n_seq,
        )

    def silu(v):
        return v / (1.0 + jnp.exp(-v))

    def finish_local(s):
        causal = lax.broadcasted_iota(jnp.int32, (length, length), 0) >= lax.broadcasted_iota(
            jnp.int32, (length, length), 1
        )
        kept = []
        for head in range(heads):
            at = slice(head * DH, (head + 1) * DH)
            k = silu(acc[s, 1, :, at]).astype(jnp.bfloat16)
            v = acc[s, 2, :, at].astype(jnp.bfloat16)
            state = lax.dot_general(k, v, (((0,), (0,)), ((), ())), preferred_element_type=jnp.float32)
            state_out[s, head] = state.astype(jnp.bfloat16)
            kept.append((k, v))

        @pl.loop(1, n_seq - c)
        def _(o):
            state_to(s, o).start()

        for head in range(heads):
            at = slice(head * DH, (head + 1) * DH)
            k, v = kept[head]
            q = silu(acc[s, 0, :, at]).astype(jnp.bfloat16)
            scores = lax.dot_general(q, k, (((1,), (1,)), ((), ())), preferred_element_type=jnp.float32)
            scores_b = jnp.where(causal, scores, 0.0).astype(jnp.bfloat16)
            queries[s, :, at] = q
            acc[s, 0, :, at] = jnp.dot(scores_b, v, preferred_element_type=jnp.float32)

    def to_owner(s):
        at = pl.ds(pl.multiple_of(d * cols, cols), cols)
        return remote(stage.at[s], out.at[0, :, at], o_send.at[s], o_recv.at[d], dp=s)

    def keep(s):
        at = pl.ds(pl.multiple_of(d * cols, cols), cols)
        return pltpu.make_async_copy(stage.at[s], out.at[0, :, at], o_sem)

    def finish_carried(s):
        @pl.when(c > 0)
        def _():
            @pl.loop(1, c + 1)
            def _(o):
                state_to(s, o).wait_recv()

            for head in range(heads):
                at = slice(head * DH, (head + 1) * DH)
                prefix = lax.fori_loop(
                    1, c + 1,
                    lambda o, total: total + state_in[o - 1, s, head].astype(jnp.float32),
                    jnp.zeros((DH, DH), jnp.float32),
                )
                acc[s, 0, :, at] += jnp.dot(
                    queries[s, :, at], prefix.astype(jnp.bfloat16),
                    preferred_element_type=jnp.float32,
                )

        for head in range(heads):
            at = slice(head * DH, (head + 1) * DH)
            attn = acc[s, 0, :, at]
            scale = lax.rsqrt(jnp.mean(attn * attn, axis=-1, keepdims=True) + 1e-06)
            stage[s, :, at] = (attn * scale * gain[:, at]).astype(jnp.bfloat16)

    def compute(t):
        i = t % TURNS

        @pl.when(t // TURNS == OWN_AT)
        def _():
            parts = []
            for n in range(SUBS):
                b = i * SUBS + n
                piece = own[:, pl.ds(pl.multiple_of(b * block, block), block)]
                parts.append(times(piece, b))
            add(d, parts)

            @pl.when(i == TURNS - 1)
            def _():
                finish_local(d)

        def one(s, up):
            blocks = (z_block(i), x_block(i), y_block(i))
            add(s, [times(tok[s, b], b) for b in blocks])

            @pl.when(i == TURNS - 1)
            def _():
                finish_local(s)

        for_sources(t // TURNS + 1, one)

    def output(t):
        @pl.when(t % TURNS == TURNS - 1)
        def _():
            @pl.when(t // TURNS == OWN_AT)
            def _():
                finish_carried(d)
                keep(d).start()

            def one(s, up):
                finish_carried(s)
                to_owner(s).start()

            for_sources(t // TURNS + 1, one)

    turns = (n_dp - 1) * TURNS
    for t in range(START):
        z_phase(t)
        if t >= LAG:
            xy_phase(t - LAG)
    own_copy.wait()
    w_copy.wait()
    for o in range(1, n_seq):
        for j in range(3):
            share(o, j).wait_recv()

    @pl.loop(START, EVEN)
    def _(t):
        z_phase(t)
        xy_phase(t - LAG)

        @pl.loop(0, 2)
        def _(n):
            @pl.when(t > START)
            def _():
                output(2 * (t - 1 - START) + n)

            compute(2 * (t - START) + n)

    @pl.loop(EVEN, turns + LAG)
    def _(t):
        @pl.when(t < turns)
        def _():
            z_phase(t)

        xy_phase(t - LAG)
        output(t - LAG - 1)
        compute(t - LAG)

    output(turns - 1)

    for o in range(1, n_seq):
        for j in range(3):
            share(o, j).wait_send()

    for i in range(TURNS):
        @pl.when(d < n_dp - 1)
        def _():
            first(i, True).wait_send()

        @pl.when(d > 0)
        def _():
            first(i, False).wait_send()

    @pl.loop(0, turns)
    def _(t):
        i = t % TURNS

        def one(s, up):
            @pl.when(d < n_dp - 1 if up else d > 0)
            def _():
                along(s, i, up).wait_send()

            to_x(s, i, z_block(i)).wait_send()
            to_y(s, i, z_block(i)).wait_send()

        for_sources(t // TURNS + 1, one)

    @pl.loop(0, n_dp)
    def _(s):
        @pl.loop(1, n_seq - c)
        def _(o):
            state_to(s, o).wait_send()

        @pl.when(s != d)
        def _():
            to_owner(s).wait_send()
            at = pl.ds(pl.multiple_of(s * cols, cols), cols)
            remote(stage.at[s], out.at[0, :, at], o_send.at[s], o_recv.at[s], dp=s).wait_recv()

    keep(d).wait()


def body(sizes, tokens, proj_weights, norm_gain):
    n_seq, n_heads, n_dp = sizes
    _, length, width = tokens.shape
    _, rows, cols = proj_weights.shape
    pieces = n_heads * SUBS
    block = width // pieces
    heads = cols // DH
    dma = pltpu.SemaphoreType.DMA
    hbm = pl.BlockSpec(memory_space=pltpu.HBM)
    flops = 2 * n_dp * length * width * 3 * cols
    return pl.pallas_call(
        functools.partial(kernel, sizes),
        out_shape=jax.ShapeDtypeStruct((1, length, n_dp * cols), jnp.bfloat16),
        in_specs=[hbm, hbm, pl.BlockSpec(memory_space=pltpu.VMEM)],
        out_specs=hbm,
        scratch_shapes=[
            pltpu.VMEM((n_dp, pieces, length, block), jnp.bfloat16),
            pltpu.VMEM((length, width), jnp.bfloat16),
            pltpu.VMEM((3, width, cols), jnp.bfloat16),
            pltpu.VMEM((n_dp, 3, length, cols), jnp.float32),
            pltpu.VMEM((n_dp, length, cols), jnp.bfloat16),
            pltpu.VMEM((n_dp, length, cols), jnp.bfloat16),
            pltpu.VMEM((n_dp, heads, DH, DH), jnp.bfloat16),
            pltpu.VMEM((n_seq - 1, n_dp, heads, DH, DH), jnp.bfloat16),
            dma, dma, dma((n_seq - 1, 3)), dma((n_seq - 1, 3)),
            dma((n_dp, TURNS)), dma((n_dp, TURNS)), dma((n_dp, TURNS)),
            dma((n_dp, TURNS)), dma((n_dp, TURNS)), dma((n_dp, TURNS)), dma((n_dp, TURNS)),
            dma((n_seq - 1, n_dp)), dma((n_seq - 1, n_dp)),
            dma((n_dp,)), dma((n_dp,)), dma,
        ],
        compiler_params=pltpu.CompilerParams(
            collective_id=0, has_side_effects=True, vmem_limit_bytes=64 * 1024 * 1024
        ),
        cost_estimate=pl.CostEstimate(
            flops=flops, bytes_accessed=2 * (tokens.size + proj_weights.size), transcendentals=0
        ),
    )(tokens, proj_weights, norm_gain.reshape(1, cols))


def solution(mesh):
    sizes = tuple(mesh.shape[name] for name in ("seq", "heads", "dp"))
    in_specs = (P("dp", "seq", None), P(None, "seq", ("heads", "dp")), P(("heads", "dp")))
    out_specs = P("dp", "seq", "heads")
    return jax.shard_map(
        functools.partial(body, sizes), mesh=mesh, in_specs=in_specs, out_specs=out_specs, check_vma=False
    )
```

```python
import functools

import jax
import jax.numpy as jnp
from jax import lax
from jax.experimental import pallas as pl
from jax.experimental.pallas import tpu as pltpu
from jax.sharding import PartitionSpec as P

DH = 128
SUBS = 3
TURNS = SUBS + 1
LAG = 2
START = 5
EVEN = 2 * START - LAG
OWN_AT = 2
MESH = pl.DeviceIdType.MESH


def kernel(
    sizes, tokens, weights, gain, out,
    tok, own, w, acc, queries, keys, values, stage, state_out, state_in,
    own_sem, w_sem, w_send, w_recv, up_send, down_send, z_recv,
    x_send, x_recv, y_send, y_recv, st_send, st_recv, o_send, o_recv, o_sem,
):
    n_seq, n_heads, n_dp = sizes
    c, h, d = lax.axis_index("seq"), lax.axis_index("heads"), lax.axis_index("dp")
    length = own.shape[0]
    rows, cols = weights.shape[1], weights.shape[2]
    block = tok.shape[3]
    heads = cols // DH
    xp = h + 1 - 2 * (h % 2)
    yp = h + 2 - 4 * (h // 2)
    across = xp + yp - h

    def remote(src, dst, send, recv, **device):
        return pltpu.make_async_remote_copy(
            src_ref=src, dst_ref=dst, send_sem=send, recv_sem=recv,
            device_id=device, device_id_type=MESH,
        )

    own_copy = pltpu.make_async_copy(tokens.at[0], own, own_sem)
    own_copy.start()
    my_rows = w.at[:, pl.ds(pl.multiple_of(c * rows, 16), rows), :]
    w_copy = pltpu.make_async_copy(weights, my_rows, w_sem)
    w_copy.start()

    barrier = pltpu.get_barrier_semaphore()
    for o in range(1, n_dp):
        pl.semaphore_signal(barrier, inc=1, device_id={"dp": (d + o) % n_dp}, device_id_type=MESH)
    for o in range(1, n_seq):
        pl.semaphore_signal(barrier, inc=1, device_id={"seq": (c + o) % n_seq}, device_id_type=MESH)
    pl.semaphore_signal(barrier, inc=1, device_id={"heads": xp}, device_id_type=MESH)
    pl.semaphore_signal(barrier, inc=1, device_id={"heads": yp}, device_id_type=MESH)
    pl.semaphore_wait(barrier, n_dp + n_seq)

    def z_block(i):
        last = i // SUBS
        return (1 - last) * (h * SUBS + SUBS - 1 - i) + last * across * SUBS

    def x_block(i):
        last = i // SUBS
        return (1 - last) * (xp * SUBS + SUBS - 1 - i) + last * (across * SUBS + 1)

    def y_block(i):
        last = i // SUBS
        return (1 - last) * (yp * SUBS + SUBS - 1 - i) + last * (across * SUBS + 2)

    def first(i, up):
        b = z_block(i)
        src = tokens.at[0, :, pl.ds(pl.multiple_of(b * block, block), block)]
        return remote(
            src, tok.at[d, b], (up_send if up else down_send).at[d, i], z_recv.at[d, i],
            dp=d + 1 if up else d - 1,
        )

    def along(s, i, up):
        b = z_block(i)
        return remote(
            tok.at[s, b], tok.at[s, b], (up_send if up else down_send).at[s, i],
            z_recv.at[s, i], dp=d + 1 if up else d - 1,
        )

    def to_x(s, i, b):
        return remote(tok.at[s, b], tok.at[s, b], x_send.at[s, i], x_recv.at[s, i], heads=xp)

    def to_y(s, i, b):
        return remote(tok.at[s, b], tok.at[s, b], y_send.at[s, i], y_recv.at[s, i], heads=yp)

    for i in range(TURNS):
        @pl.when(d < n_dp - 1)
        def _():
            first(i, True).start()

        @pl.when(d > 0)
        def _():
            first(i, False).start()

    def share(o, j):
        return remote(
            weights.at[j], my_rows.at[j], w_send.at[o - 1, j], w_recv.at[o - 1, j],
            seq=(c + o) % n_seq,
        )

    for o in range(1, n_seq):
        for j in range(3):
            share(o, j).start()

    acc[...] = jnp.zeros_like(acc)

    def for_sources(k, do):
        @pl.when(d - k >= 0)
        def _():
            do(d - k, True)

        @pl.when(d + k < n_dp)
        def _():
            do(d + k, False)

    def z_phase(t):
        i = t % TURNS

        def one(s, up):
            b = z_block(i)
            along(s, i, up).wait_recv()
            @pl.when(d < n_dp - 1 if up else d > 0)
            def _():
                along(s, i, up).start()

            @pl.when(i < SUBS)
            def _():
                to_x(s, i, b).start()
                to_y(s, i, b).start()

        for_sources(t // TURNS + 1, one)

    def xy_phase(t):
        i = t % TURNS

        def one(s, up):
            to_x(s, i, x_block(i)).wait_recv()

            @pl.when(i == 0)
            def _():
                to_y(s, SUBS, x_block(0)).start()

            to_y(s, i, y_block(i)).wait_recv()

            @pl.when(i == 1)
            def _():
                to_x(s, SUBS, y_block(1)).start()

        for_sources(t // TURNS + 1, one)

    def rows_of(s, blocks):
        return jnp.concatenate([tok[s, b] for b in blocks], axis=1)

    def own_rows(blocks):
        return jnp.concatenate(
            [own[:, pl.ds(pl.multiple_of(b * block, block), block)] for b in blocks], axis=1
        )

    def multiply(i, blocks, parts):
        piece = jnp.concatenate([rows for _, rows in parts], axis=0)

        def add(j):
            k_rows = [pl.ds(pl.multiple_of(b * block, block), block) for b in blocks]
            weight = jnp.concatenate([w[j, at, :] for at in k_rows], axis=0)
            product = jnp.dot(piece, weight, preferred_element_type=jnp.float32)
            for n, (s, _) in enumerate(parts):
                acc[s, j] += product[n * length:(n + 1) * length]

        add(1)
        add(2)

        @pl.when(i == TURNS - 1)
        def _():
            for s, _ in parts:
                make_state(s)

        add(0)

        @pl.when(i == TURNS - 1)
        def _():
            for s, _ in parts:
                finish_local(s)

    def state_to(s, o):
        return remote(
            state_out.at[s], state_in.at[o - 1, s], st_send.at[o - 1, s], st_recv.at[o - 1, s],
            seq=(c + o) % n_seq,
        )

    def silu(v):
        return v / (1.0 + jnp.exp(-v))

    def make_state(s):
        for head in range(heads):
            at = slice(head * DH, (head + 1) * DH)
            k = silu(acc[s, 1, :, at]).astype(jnp.bfloat16)
            v = acc[s, 2, :, at].astype(jnp.bfloat16)
            state = lax.dot_general(k, v, (((0,), (0,)), ((), ())), preferred_element_type=jnp.float32)
            state_out[s, head] = state.astype(jnp.bfloat16)
            keys[s, :, at] = k
            values[s, :, at] = v

        @pl.loop(1, n_seq - c)
        def _(o):
            state_to(s, o).start()

    def finish_local(s):
        causal = lax.broadcasted_iota(jnp.int32, (length, length), 0) >= lax.broadcasted_iota(
            jnp.int32, (length, length), 1
        )
        for head in range(heads):
            at = slice(head * DH, (head + 1) * DH)
            q = silu(acc[s, 0, :, at]).astype(jnp.bfloat16)
            scores = lax.dot_general(
                q, keys[s, :, at], (((1,), (1,)), ((), ())), preferred_element_type=jnp.float32
            )
            scores_b = jnp.where(causal, scores, 0.0).astype(jnp.bfloat16)
            queries[s, :, at] = q
            acc[s, 0, :, at] = jnp.dot(
                scores_b, values[s, :, at], preferred_element_type=jnp.float32
            )

    def to_owner(s):
        at = pl.ds(pl.multiple_of(d * cols, cols), cols)
        return remote(stage.at[s], out.at[0, :, at], o_send.at[s], o_recv.at[d], dp=s)

    def keep(s):
        at = pl.ds(pl.multiple_of(d * cols, cols), cols)
        return pltpu.make_async_copy(stage.at[s], out.at[0, :, at], o_sem)

    def finish_carried(s):
        @pl.when(c > 0)
        def _():
            @pl.loop(1, c + 1)
            def _(o):
                state_to(s, o).wait_recv()

            for head in range(heads):
                at = slice(head * DH, (head + 1) * DH)
                prefix = lax.fori_loop(
                    1, c + 1,
                    lambda o, total: total + state_in[o - 1, s, head].astype(jnp.float32),
                    jnp.zeros((DH, DH), jnp.float32),
                )
                acc[s, 0, :, at] += jnp.dot(
                    queries[s, :, at], prefix.astype(jnp.bfloat16),
                    preferred_element_type=jnp.float32,
                )

        for head in range(heads):
            at = slice(head * DH, (head + 1) * DH)
            attn = acc[s, 0, :, at]
            scale = lax.rsqrt(jnp.mean(attn * attn, axis=-1, keepdims=True) + 1e-06)
            stage[s, :, at] = (attn * scale * gain[:, at]).astype(jnp.bfloat16)

    def compute(t):
        i = t % TURNS
        k = t // TURNS + 1
        blocks = (z_block(i), x_block(i), y_block(i))
        below = (d + n_dp - k) // n_dp
        above = (2 * n_dp - 1 - d - k) // n_dp

        @pl.when(below + above == 2)
        def _():
            multiply(i, blocks, [(s, rows_of(s, blocks)) for s in (d - k, d + k)])

        @pl.when(below + above == 1)
        def _():
            s = d + k - 2 * k * below

            @pl.when(k == OWN_AT)
            def _():
                multiply(i, blocks, [(d, own_rows(blocks)), (s, rows_of(s, blocks))])

            @pl.when(k != OWN_AT)
            def _():
                multiply(i, blocks, [(s, rows_of(s, blocks))])

        if 2 * OWN_AT < n_dp:
            @pl.when((k == OWN_AT) & (below + above != 1))
            def _():
                multiply(i, blocks, [(d, own_rows(blocks))])

    def output(t):
        @pl.when(t % TURNS == TURNS - 1)
        def _():
            @pl.when(t // TURNS + 1 == OWN_AT)
            def _():
                finish_carried(d)
                keep(d).start()

            def one(s, up):
                finish_carried(s)
                to_owner(s).start()

            for_sources(t // TURNS + 1, one)

    turns = (n_dp - 1) * TURNS
    for t in range(START):
        z_phase(t)
        if t >= LAG:
            xy_phase(t - LAG)
    own_copy.wait()
    w_copy.wait()
    for o in range(1, n_seq):
        for j in range(3):
            share(o, j).wait_recv()

    @pl.loop(START, EVEN)
    def _(t):
        z_phase(t)
        xy_phase(t - LAG)

        @pl.loop(0, 2)
        def _(n):
            @pl.when(t > START)
            def _():
                output(2 * (t - 1 - START) + n)

            compute(2 * (t - START) + n)

    late = turns - TURNS

    @pl.loop(EVEN, late + 1)
    def _(t):
        z_phase(t)
        xy_phase(t - LAG)
        output(t - LAG - 1)
        compute(t - LAG)

    xy_phase(late - 1)
    compute(late - 1)

    @pl.loop(late + 1, turns + 1)
    def _(t):
        @pl.when(t < turns)
        def _():
            z_phase(t)

        xy_phase(t - 1)
        output(t - 2)
        compute(t - 1)

    output(turns - 1)

    for o in range(1, n_seq):
        for j in range(3):
            share(o, j).wait_send()

    for i in range(TURNS):
        @pl.when(d < n_dp - 1)
        def _():
            first(i, True).wait_send()

        @pl.when(d > 0)
        def _():
            first(i, False).wait_send()

    @pl.loop(0, turns)
    def _(t):
        i = t % TURNS

        def one(s, up):
            @pl.when(d < n_dp - 1 if up else d > 0)
            def _():
                along(s, i, up).wait_send()

            to_x(s, i, z_block(i)).wait_send()
            to_y(s, i, z_block(i)).wait_send()

        for_sources(t // TURNS + 1, one)

    @pl.loop(0, n_dp)
    def _(s):
        @pl.loop(1, n_seq - c)
        def _(o):
            state_to(s, o).wait_send()

        @pl.when(s != d)
        def _():
            to_owner(s).wait_send()
            at = pl.ds(pl.multiple_of(s * cols, cols), cols)
            remote(stage.at[s], out.at[0, :, at], o_send.at[s], o_recv.at[s], dp=s).wait_recv()

    keep(d).wait()


def body(sizes, tokens, proj_weights, norm_gain):
    n_seq, n_heads, n_dp = sizes
    _, length, width = tokens.shape
    _, rows, cols = proj_weights.shape
    pieces = n_heads * SUBS
    block = width // pieces
    heads = cols // DH
    dma = pltpu.SemaphoreType.DMA
    hbm = pl.BlockSpec(memory_space=pltpu.HBM)
    flops = 2 * n_dp * length * width * 3 * cols
    return pl.pallas_call(
        functools.partial(kernel, sizes),
        out_shape=jax.ShapeDtypeStruct((1, length, n_dp * cols), jnp.bfloat16),
        in_specs=[hbm, hbm, pl.BlockSpec(memory_space=pltpu.VMEM)],
        out_specs=hbm,
        scratch_shapes=[
            pltpu.VMEM((n_dp, pieces, length, block), jnp.bfloat16),
            pltpu.VMEM((length, width), jnp.bfloat16),
            pltpu.VMEM((3, width, cols), jnp.bfloat16),
            pltpu.VMEM((n_dp, 3, length, cols), jnp.float32),
            pltpu.VMEM((n_dp, length, cols), jnp.bfloat16),
            pltpu.VMEM((n_dp, length, cols), jnp.bfloat16),
            pltpu.VMEM((n_dp, length, cols), jnp.bfloat16),
            pltpu.VMEM((n_dp, length, cols), jnp.bfloat16),
            pltpu.VMEM((n_dp, heads, DH, DH), jnp.bfloat16),
            pltpu.VMEM((n_seq - 1, n_dp, heads, DH, DH), jnp.bfloat16),
            dma, dma, dma((n_seq - 1, 3)), dma((n_seq - 1, 3)),
            dma((n_dp, TURNS)), dma((n_dp, TURNS)), dma((n_dp, TURNS)),
            dma((n_dp, TURNS)), dma((n_dp, TURNS)), dma((n_dp, TURNS)), dma((n_dp, TURNS)),
            dma((n_seq - 1, n_dp)), dma((n_seq - 1, n_dp)),
            dma((n_dp,)), dma((n_dp,)), dma,
        ],
        compiler_params=pltpu.CompilerParams(
            collective_id=0, has_side_effects=True, vmem_limit_bytes=(64 * 1024 - 512) * 1024
        ),
        cost_estimate=pl.CostEstimate(
            flops=flops, bytes_accessed=2 * (tokens.size + proj_weights.size), transcendentals=0
        ),
    )(tokens, proj_weights, norm_gain.reshape(1, cols))


def solution(mesh):
    sizes = tuple(mesh.shape[name] for name in ("seq", "heads", "dp"))
    in_specs = (P("dp", "seq", None), P(None, "seq", ("heads", "dp")), P(("heads", "dp")))
    out_specs = P("dp", "seq", "heads")
    return jax.shard_map(
        functools.partial(body, sizes), mesh=mesh, in_specs=in_specs, out_specs=out_specs, check_vma=False
    )
```

```python
import functools

import jax
import jax.numpy as jnp
from jax import lax
from jax.experimental import pallas as pl
from jax.experimental.pallas import tpu as pltpu
from jax.sharding import PartitionSpec as P

DH = 128
SUBS = 3
TURNS = SUBS + 1
LAG = 2
OWN_AT = 2
MESH = pl.DeviceIdType.MESH


def kernel(
    sizes, tokens, weights, gain, out,
    tok, own, w, acc, queries, keys, values, stage, state_out, state_in,
    own_sem, w_sem, w_send, w_recv, up_send, down_send, z_recv,
    x_send, x_recv, y_send, y_recv, st_send, st_recv, o_send, o_recv, o_sem,
):
    n_seq, n_heads, n_dp = sizes
    c, h, d = lax.axis_index("seq"), lax.axis_index("heads"), lax.axis_index("dp")
    length = own.shape[0]
    rows, cols = weights.shape[1], weights.shape[2]
    block = tok.shape[3]
    heads = cols // DH
    xp = h + 1 - 2 * (h % 2)
    yp = h + 2 - 4 * (h // 2)
    across = xp + yp - h

    def remote(src, dst, send, recv, **device):
        return pltpu.make_async_remote_copy(
            src_ref=src, dst_ref=dst, send_sem=send, recv_sem=recv,
            device_id=device, device_id_type=MESH,
        )

    own_copy = pltpu.make_async_copy(tokens.at[0], own, own_sem)
    own_copy.start()
    my_rows = w.at[:, pl.ds(pl.multiple_of(c * rows, 16), rows), :]
    w_copy = pltpu.make_async_copy(weights, my_rows, w_sem)
    w_copy.start()

    barrier = pltpu.get_barrier_semaphore()
    for o in range(1, n_dp):
        pl.semaphore_signal(barrier, inc=1, device_id={"dp": (d + o) % n_dp}, device_id_type=MESH)
    for o in range(1, n_seq):
        pl.semaphore_signal(barrier, inc=1, device_id={"seq": (c + o) % n_seq}, device_id_type=MESH)
    pl.semaphore_signal(barrier, inc=1, device_id={"heads": xp}, device_id_type=MESH)
    pl.semaphore_signal(barrier, inc=1, device_id={"heads": yp}, device_id_type=MESH)
    pl.semaphore_wait(barrier, n_dp + n_seq)

    def z_block(i):
        last = i // SUBS
        return (1 - last) * (h * SUBS + SUBS - 1 - i) + last * across * SUBS

    def x_block(i):
        last = i // SUBS
        return (1 - last) * (xp * SUBS + SUBS - 1 - i) + last * (across * SUBS + 1)

    def y_block(i):
        last = i // SUBS
        return (1 - last) * (yp * SUBS + SUBS - 1 - i) + last * (across * SUBS + 2)

    def first(i, up):
        b = z_block(i)
        src = tokens.at[0, :, pl.ds(pl.multiple_of(b * block, block), block)]
        return remote(
            src, tok.at[d, b], (up_send if up else down_send).at[d, i], z_recv.at[d, i],
            dp=d + 1 if up else d - 1,
        )

    def along(s, i, up):
        b = z_block(i)
        return remote(
            tok.at[s, b], tok.at[s, b], (up_send if up else down_send).at[s, i],
            z_recv.at[s, i], dp=d + 1 if up else d - 1,
        )

    def to_x(s, i, b):
        return remote(tok.at[s, b], tok.at[s, b], x_send.at[s, i], x_recv.at[s, i], heads=xp)

    def to_y(s, i, b):
        return remote(tok.at[s, b], tok.at[s, b], y_send.at[s, i], y_recv.at[s, i], heads=yp)

    for i in range(TURNS):
        @pl.when(d < n_dp - 1)
        def _():
            first(i, True).start()

        @pl.when(d > 0)
        def _():
            first(i, False).start()

    part = min(rows, block)
    parts = rows // part

    def share(o, n):
        at = pl.ds(pl.multiple_of(n // 3 * part, 16), part)
        return remote(
            weights.at[n % 3, at], my_rows.at[n % 3, at], w_send.at[o - 1, n], w_recv.at[o - 1, n],
            seq=(c + o) % n_seq,
        )

    for o in range(1, n_seq):
        @pl.loop(0, 3 * parts)
        def _(n):
            share(o, n).start()

    acc[...] = jnp.zeros_like(acc)

    def for_sources(k, do):
        @pl.when(d - k >= 0)
        def _():
            do(d - k, True)

        @pl.when(d + k < n_dp)
        def _():
            do(d + k, False)

    def z_phase(t):
        i = t % TURNS

        def one(s, up):
            b = z_block(i)
            along(s, i, up).wait_recv()
            @pl.when(d < n_dp - 1 if up else d > 0)
            def _():
                along(s, i, up).start()

            @pl.when(i < SUBS)
            def _():
                to_x(s, i, b).start()
                to_y(s, i, b).start()

        for_sources(t // TURNS + 1, one)

    def xy_phase(t):
        i = t % TURNS

        def one(s, up):
            to_x(s, i, x_block(i)).wait_recv()

            @pl.when(i == 0)
            def _():
                to_y(s, SUBS, x_block(0)).start()

            to_y(s, i, y_block(i)).wait_recv()

            @pl.when(i == 1)
            def _():
                to_x(s, SUBS, y_block(1)).start()

        for_sources(t // TURNS + 1, one)

    def rows_of(s, blocks):
        return jnp.concatenate([tok[s, b] for b in blocks], axis=1)

    def own_rows(blocks):
        return jnp.concatenate(
            [own[:, pl.ds(pl.multiple_of(b * block, block), block)] for b in blocks], axis=1
        )

    def multiply(i, blocks, group):
        piece = jnp.concatenate([rows for _, rows in group], axis=0)

        def add(j):
            k_rows = [pl.ds(pl.multiple_of(b * block, block), block) for b in blocks]
            weight = jnp.concatenate([w[j, at, :] for at in k_rows], axis=0)
            product = jnp.dot(piece, weight, preferred_element_type=jnp.float32)
            for n, (s, _) in enumerate(group):
                acc[s, j] += product[n * length:(n + 1) * length]

        add(1)
        add(2)

        @pl.when(i == TURNS - 1)
        def _():
            for s, _ in group:
                make_state(s)

        add(0)

        @pl.when(i == TURNS - 1)
        def _():
            for s, _ in group:
                finish_local(s)

    def state_to(s, o):
        return remote(
            state_out.at[s], state_in.at[o - 1, s], st_send.at[o - 1, s], st_recv.at[o - 1, s],
            seq=(c + o) % n_seq,
        )

    def silu(v):
        return v / (1.0 + jnp.exp(-v))

    def make_state(s):
        for head in range(heads):
            at = slice(head * DH, (head + 1) * DH)
            k = silu(acc[s, 1, :, at]).astype(jnp.bfloat16)
            v = acc[s, 2, :, at].astype(jnp.bfloat16)
            state = lax.dot_general(k, v, (((0,), (0,)), ((), ())), preferred_element_type=jnp.float32)
            state_out[s, head] = state.astype(jnp.bfloat16)
            keys[s, :, at] = k
            values[s, :, at] = v

        @pl.loop(1, n_seq - c)
        def _(o):
            state_to(s, o).start()

    def finish_local(s):
        causal = lax.broadcasted_iota(jnp.int32, (length, length), 0) >= lax.broadcasted_iota(
            jnp.int32, (length, length), 1
        )
        for head in range(heads):
            at = slice(head * DH, (head + 1) * DH)
            q = silu(acc[s, 0, :, at]).astype(jnp.bfloat16)
            scores = lax.dot_general(
                q, keys[s, :, at], (((1,), (1,)), ((), ())), preferred_element_type=jnp.float32
            )
            scores_b = jnp.where(causal, scores, 0.0).astype(jnp.bfloat16)
            queries[s, :, at] = q
            acc[s, 0, :, at] = jnp.dot(
                scores_b, values[s, :, at], preferred_element_type=jnp.float32
            )

    def to_owner(s):
        at = pl.ds(pl.multiple_of(d * cols, cols), cols)
        return remote(stage.at[s], out.at[0, :, at], o_send.at[s], o_recv.at[d], dp=s)

    def keep(s):
        at = pl.ds(pl.multiple_of(d * cols, cols), cols)
        return pltpu.make_async_copy(stage.at[s], out.at[0, :, at], o_sem)

    def finish_carried(s):
        @pl.when(c > 0)
        def _():
            @pl.loop(1, c + 1)
            def _(o):
                state_to(s, o).wait_recv()

            for head in range(heads):
                at = slice(head * DH, (head + 1) * DH)
                prefix = lax.fori_loop(
                    1, c + 1,
                    lambda o, total: total + state_in[o - 1, s, head].astype(jnp.float32),
                    jnp.zeros((DH, DH), jnp.float32),
                )
                acc[s, 0, :, at] += jnp.dot(
                    queries[s, :, at], prefix.astype(jnp.bfloat16),
                    preferred_element_type=jnp.float32,
                )

        for head in range(heads):
            at = slice(head * DH, (head + 1) * DH)
            attn = acc[s, 0, :, at]
            scale = lax.rsqrt(jnp.mean(attn * attn, axis=-1, keepdims=True) + 1e-06)
            stage[s, :, at] = (attn * scale * gain[:, at]).astype(jnp.bfloat16)

    def compute(t):
        i = t % TURNS
        k = t // TURNS + 1
        blocks = (z_block(i), x_block(i), y_block(i))
        below = (d + n_dp - k) // n_dp
        above = (2 * n_dp - 1 - d - k) // n_dp

        @pl.when(below + above == 2)
        def _():
            multiply(i, blocks, [(s, rows_of(s, blocks)) for s in (d - k, d + k)])

        @pl.when(below + above == 1)
        def _():
            s = d + k - 2 * k * below

            @pl.when(k == OWN_AT)
            def _():
                multiply(i, blocks, [(d, own_rows(blocks)), (s, rows_of(s, blocks))])

            @pl.when(k != OWN_AT)
            def _():
                multiply(i, blocks, [(s, rows_of(s, blocks))])

        if 2 * OWN_AT < n_dp:
            @pl.when((k == OWN_AT) & (below + above != 1))
            def _():
                multiply(i, blocks, [(d, own_rows(blocks))])

    def output(t):
        @pl.when(t % TURNS == TURNS - 1)
        def _():
            @pl.when(t // TURNS + 1 == OWN_AT)
            def _():
                finish_carried(d)
                keep(d).start()

            def one(s, up):
                finish_carried(s)
                to_owner(s).start()

            for_sources(t // TURNS + 1, one)

    turns = (n_dp - 1) * TURNS
    late = turns - TURNS

    @pl.loop(0, late + 1)
    def _(t):
        z_phase(t)

        @pl.when(t >= LAG)
        def _():
            xy_phase(t - LAG)

    xy_phase(late - 1)
    own_copy.wait()
    w_copy.wait()
    for o in range(1, n_seq):
        @pl.loop(0, 3 * parts)
        def _(n):
            share(o, n).wait_recv()

    step = turns // TURNS

    @pl.loop(0, TURNS)
    def _(n):
        t = late + 1 + n

        @pl.when(t < turns)
        def _():
            z_phase(t)

        xy_phase(t - 1)

        @pl.loop(0, step)
        def _(m):
            @pl.when(n > 0)
            def _():
                output((n - 1) * step + m)

        @pl.loop(0, step)
        def _(m):
            compute(n * step + m)

    output(turns - 1)

    for o in range(1, n_seq):
        @pl.loop(0, 3 * parts)
        def _(n):
            share(o, n).wait_send()

    for i in range(TURNS):
        @pl.when(d < n_dp - 1)
        def _():
            first(i, True).wait_send()

        @pl.when(d > 0)
        def _():
            first(i, False).wait_send()

    @pl.loop(0, turns)
    def _(t):
        i = t % TURNS

        def one(s, up):
            @pl.when(d < n_dp - 1 if up else d > 0)
            def _():
                along(s, i, up).wait_send()

            to_x(s, i, z_block(i)).wait_send()
            to_y(s, i, z_block(i)).wait_send()

        for_sources(t // TURNS + 1, one)

    @pl.loop(0, n_dp)
    def _(s):
        @pl.loop(1, n_seq - c)
        def _(o):
            state_to(s, o).wait_send()

        @pl.when(s != d)
        def _():
            to_owner(s).wait_send()
            at = pl.ds(pl.multiple_of(s * cols, cols), cols)
            remote(stage.at[s], out.at[0, :, at], o_send.at[s], o_recv.at[s], dp=s).wait_recv()

    keep(d).wait()


def body(sizes, tokens, proj_weights, norm_gain):
    n_seq, n_heads, n_dp = sizes
    _, length, width = tokens.shape
    _, rows, cols = proj_weights.shape
    pieces = n_heads * SUBS
    block = width // pieces
    heads = cols // DH
    copies = 3 * (rows // min(rows, block))
    dma = pltpu.SemaphoreType.DMA
    hbm = pl.BlockSpec(memory_space=pltpu.HBM)
    flops = 2 * n_dp * length * width * 3 * cols
    return pl.pallas_call(
        functools.partial(kernel, sizes),
        out_shape=jax.ShapeDtypeStruct((1, length, n_dp * cols), jnp.bfloat16),
        in_specs=[hbm, hbm, pl.BlockSpec(memory_space=pltpu.VMEM)],
        out_specs=hbm,
        scratch_shapes=[
            pltpu.VMEM((n_dp, pieces, length, block), jnp.bfloat16),
            pltpu.VMEM((length, width), jnp.bfloat16),
            pltpu.VMEM((3, width, cols), jnp.bfloat16),
            pltpu.VMEM((n_dp, 3, length, cols), jnp.float32),
            pltpu.VMEM((n_dp, length, cols), jnp.bfloat16),
            pltpu.VMEM((n_dp, length, cols), jnp.bfloat16),
            pltpu.VMEM((n_dp, length, cols), jnp.bfloat16),
            pltpu.VMEM((n_dp, length, cols), jnp.bfloat16),
            pltpu.VMEM((n_dp, heads, DH, DH), jnp.bfloat16),
            pltpu.VMEM((n_seq - 1, n_dp, heads, DH, DH), jnp.bfloat16),
            dma, dma, dma((n_seq - 1, copies)), dma((n_seq - 1, copies)),
            dma((n_dp, TURNS)), dma((n_dp, TURNS)), dma((n_dp, TURNS)),
            dma((n_dp, TURNS)), dma((n_dp, TURNS)), dma((n_dp, TURNS)), dma((n_dp, TURNS)),
            dma((n_seq - 1, n_dp)), dma((n_seq - 1, n_dp)),
            dma((n_dp,)), dma((n_dp,)), dma,
        ],
        compiler_params=pltpu.CompilerParams(
            collective_id=0, has_side_effects=True, vmem_limit_bytes=(64 * 1024 - 512) * 1024
        ),
        cost_estimate=pl.CostEstimate(
            flops=flops, bytes_accessed=2 * (tokens.size + proj_weights.size), transcendentals=0
        ),
    )(tokens, proj_weights, norm_gain.reshape(1, cols))


def solution(mesh):
    sizes = tuple(mesh.shape[name] for name in ("seq", "heads", "dp"))
    in_specs = (P("dp", "seq", None), P(None, "seq", ("heads", "dp")), P(("heads", "dp")))
    out_specs = P("dp", "seq", "heads")
    return jax.shard_map(
        functools.partial(body, sizes), mesh=mesh, in_specs=in_specs, out_specs=out_specs, check_vma=False
    )
```

```python
import functools

import jax
import jax.numpy as jnp
from jax import lax
from jax.experimental import pallas as pl
from jax.experimental.pallas import tpu as pltpu
from jax.sharding import PartitionSpec as P

DH = 128
SUBS = 3
TURNS = SUBS + 1
LAG = 2
MESH = pl.DeviceIdType.MESH


def kernel(
    sizes, tokens, weights, gain, out,
    tok, own, w, acc, queries, keys, values, stage, state_out, state_in,
    own_sem, w_sem, w_send, w_recv, up_send, down_send, z_recv,
    x_send, x_recv, y_send, y_recv, st_send, st_recv, o_send, o_recv, o_sem,
):
    n_seq, n_heads, n_dp = sizes
    c, h, d = lax.axis_index("seq"), lax.axis_index("heads"), lax.axis_index("dp")
    length = own.shape[0]
    rows, cols = weights.shape[1], weights.shape[2]
    block = tok.shape[3]
    heads = cols // DH
    xp = h + 1 - 2 * (h % 2)
    yp = h + 2 - 4 * (h // 2)
    across = xp + yp - h

    def remote(src, dst, send, recv, **device):
        return pltpu.make_async_remote_copy(
            src_ref=src, dst_ref=dst, send_sem=send, recv_sem=recv,
            device_id=device, device_id_type=MESH,
        )

    own_copy = pltpu.make_async_copy(tokens.at[0], own, own_sem)
    own_copy.start()
    my_rows = w.at[:, pl.ds(pl.multiple_of(c * rows, 16), rows), :]
    w_copy = pltpu.make_async_copy(weights, my_rows, w_sem)
    w_copy.start()

    barrier = pltpu.get_barrier_semaphore()
    for o in range(1, n_dp):
        pl.semaphore_signal(barrier, inc=1, device_id={"dp": (d + o) % n_dp}, device_id_type=MESH)
    for o in range(1, n_seq):
        pl.semaphore_signal(barrier, inc=1, device_id={"seq": (c + o) % n_seq}, device_id_type=MESH)
    pl.semaphore_signal(barrier, inc=1, device_id={"heads": xp}, device_id_type=MESH)
    pl.semaphore_signal(barrier, inc=1, device_id={"heads": yp}, device_id_type=MESH)
    pl.semaphore_wait(barrier, n_dp + n_seq)

    def z_block(i):
        last = i // SUBS
        return (1 - last) * (h * SUBS + SUBS - 1 - i) + last * across * SUBS

    def x_block(i):
        last = i // SUBS
        return (1 - last) * (xp * SUBS + SUBS - 1 - i) + last * (across * SUBS + 1)

    def y_block(i):
        last = i // SUBS
        return (1 - last) * (yp * SUBS + SUBS - 1 - i) + last * (across * SUBS + 2)

    def first(i, up):
        b = z_block(i)
        src = tokens.at[0, :, pl.ds(pl.multiple_of(b * block, block), block)]
        return remote(
            src, tok.at[d, b], (up_send if up else down_send).at[d, i], z_recv.at[d, i],
            dp=d + 1 if up else d - 1,
        )

    def along(s, i, up):
        b = z_block(i)
        return remote(
            tok.at[s, b], tok.at[s, b], (up_send if up else down_send).at[s, i],
            z_recv.at[s, i], dp=d + 1 if up else d - 1,
        )

    def to_x(s, i, b):
        return remote(tok.at[s, b], tok.at[s, b], x_send.at[s, i], x_recv.at[s, i], heads=xp)

    def to_y(s, i, b):
        return remote(tok.at[s, b], tok.at[s, b], y_send.at[s, i], y_recv.at[s, i], heads=yp)

    for i in range(TURNS):
        @pl.when(d < n_dp - 1)
        def _():
            first(i, True).start()

        @pl.when(d > 0)
        def _():
            first(i, False).start()

    part = min(rows, block)
    parts = rows // part

    def share(o, n):
        at = pl.ds(pl.multiple_of(n // 3 * part, 16), part)
        return remote(
            weights.at[n % 3, at], my_rows.at[n % 3, at], w_send.at[o - 1, n], w_recv.at[o - 1, n],
            seq=(c + o) % n_seq,
        )

    for o in range(1, n_seq):
        @pl.loop(0, 3 * parts)
        def _(n):
            share(o, n).start()

    acc[...] = jnp.zeros_like(acc)

    def for_sources(k, do):
        @pl.when(d - k >= 0)
        def _():
            do(d - k, True)

        @pl.when(d + k < n_dp)
        def _():
            do(d + k, False)

    def z_phase(t):
        i = t % TURNS

        def one(s, up):
            b = z_block(i)
            along(s, i, up).wait_recv()
            @pl.when(d < n_dp - 1 if up else d > 0)
            def _():
                along(s, i, up).start()

            @pl.when(i < SUBS)
            def _():
                to_x(s, i, b).start()
                to_y(s, i, b).start()

        for_sources(t // TURNS + 1, one)

    def xy_phase(t):
        i = t % TURNS

        def one(s, up):
            to_x(s, i, x_block(i)).wait_recv()

            @pl.when(i == 0)
            def _():
                to_y(s, SUBS, x_block(0)).start()

            to_y(s, i, y_block(i)).wait_recv()

            @pl.when(i == 1)
            def _():
                to_x(s, SUBS, y_block(1)).start()

        for_sources(t // TURNS + 1, one)

    def rows_of(s, blocks):
        return jnp.concatenate([tok[s, b] for b in blocks], axis=1)

    def own_rows(blocks):
        return jnp.concatenate(
            [own[:, pl.ds(pl.multiple_of(b * block, block), block)] for b in blocks], axis=1
        )

    def multiply(i, blocks, group):
        piece = jnp.concatenate([rows for _, rows in group], axis=0)

        def add(j):
            k_rows = [pl.ds(pl.multiple_of(b * block, block), block) for b in blocks]
            weight = jnp.concatenate([w[j, at, :] for at in k_rows], axis=0)
            product = jnp.dot(piece, weight, preferred_element_type=jnp.float32)
            for n, (s, _) in enumerate(group):
                acc[s, j] += product[n * length:(n + 1) * length]

        add(1)
        add(2)

        @pl.when(i == TURNS - 1)
        def _():
            for s, _ in group:
                make_state(s)

        add(0)

        @pl.when(i == TURNS - 1)
        def _():
            for s, _ in group:
                finish_local(s)

    def state_to(s, o):
        return remote(
            state_out.at[s], state_in.at[o - 1, s], st_send.at[o - 1, s], st_recv.at[o - 1, s],
            seq=(c + o) % n_seq,
        )

    def silu(v):
        return v / (1.0 + jnp.exp(-v))

    def make_state(s):
        for head in range(heads):
            at = slice(head * DH, (head + 1) * DH)
            k = silu(acc[s, 1, :, at]).astype(jnp.bfloat16)
            v = acc[s, 2, :, at].astype(jnp.bfloat16)
            state = lax.dot_general(k, v, (((0,), (0,)), ((), ())), preferred_element_type=jnp.float32)
            state_out[s, head] = state.astype(jnp.bfloat16)
            keys[s, :, at] = k
            values[s, :, at] = v

        @pl.loop(1, n_seq - c)
        def _(o):
            state_to(s, o).start()

    def finish_local(s):
        causal = lax.broadcasted_iota(jnp.int32, (length, length), 0) >= lax.broadcasted_iota(
            jnp.int32, (length, length), 1
        )
        for head in range(heads):
            at = slice(head * DH, (head + 1) * DH)
            q = silu(acc[s, 0, :, at]).astype(jnp.bfloat16)
            scores = lax.dot_general(
                q, keys[s, :, at], (((1,), (1,)), ((), ())), preferred_element_type=jnp.float32
            )
            scores_b = jnp.where(causal, scores, 0.0).astype(jnp.bfloat16)
            queries[s, :, at] = q
            acc[s, 0, :, at] = jnp.dot(
                scores_b, values[s, :, at], preferred_element_type=jnp.float32
            )

    def to_owner(s):
        at = pl.ds(pl.multiple_of(d * cols, cols), cols)
        return remote(stage.at[s], out.at[0, :, at], o_send.at[s], o_recv.at[d], dp=s)

    def keep(s):
        at = pl.ds(pl.multiple_of(d * cols, cols), cols)
        return pltpu.make_async_copy(stage.at[s], out.at[0, :, at], o_sem)

    def finish_carried(s):
        @pl.when(c > 0)
        def _():
            @pl.loop(1, c + 1)
            def _(o):
                state_to(s, o).wait_recv()

            for head in range(heads):
                at = slice(head * DH, (head + 1) * DH)
                prefix = lax.fori_loop(
                    1, c + 1,
                    lambda o, total: total + state_in[o - 1, s, head].astype(jnp.float32),
                    jnp.zeros((DH, DH), jnp.float32),
                )
                acc[s, 0, :, at] += jnp.dot(
                    queries[s, :, at], prefix.astype(jnp.bfloat16),
                    preferred_element_type=jnp.float32,
                )

        for head in range(heads):
            at = slice(head * DH, (head + 1) * DH)
            attn = acc[s, 0, :, at]
            scale = lax.rsqrt(jnp.mean(attn * attn, axis=-1, keepdims=True) + 1e-06)
            stage[s, :, at] = (attn * scale * gain[:, at]).astype(jnp.bfloat16)

    def compute(t):
        i = t % TURNS
        k = t // TURNS + 1
        blocks = (z_block(i), x_block(i), y_block(i))
        below = (d + n_dp - k) // n_dp
        above = (2 * n_dp - 1 - d - k) // n_dp

        @pl.when(below + above == 2)
        def _():
            multiply(i, blocks, [(s, rows_of(s, blocks)) for s in (d - k, d + k)])

        @pl.when(below + above == 1)
        def _():
            s = d + k - 2 * k * below

            multiply(i, blocks, [(s, rows_of(s, blocks))])

    def compute_own(i):
        blocks = [i * SUBS + n for n in range(SUBS)]
        multiply(i, blocks, [(d, own_rows(blocks))])

    def output(t):
        @pl.when(t % TURNS == TURNS - 1)
        def _():
            def one(s, up):
                finish_carried(s)
                to_owner(s).start()

            for_sources(t // TURNS + 1, one)

    turns = (n_dp - 1) * TURNS
    late = turns - TURNS

    @pl.loop(0, late - TURNS)
    def _(t):
        z_phase(t)

    own_copy.wait()
    w_copy.wait()
    for o in range(1, n_seq):
        @pl.loop(0, 3 * parts)
        def _(n):
            share(o, n).wait_recv()

    @pl.loop(late - TURNS, late)
    def _(t):
        z_phase(t)
        compute_own(t - late + TURNS)

        @pl.when(t >= late - LAG)
        def _():
            xy_phase(t - late + LAG)
            compute(t - late + LAG)

    @pl.loop(late, late + (turns - LAG) // 2)
    def _(t):
        done = LAG + 2 * (t - late)

        @pl.when(t < turns)
        def _():
            z_phase(t)

        @pl.when(t == late)
        def _():
            finish_carried(d)
            keep(d).start()

        @pl.loop(0, 2)
        def _(n):
            @pl.when(t > late)
            def _():
                output(done - 2 + n)

            xy_phase(done + n)
            compute(done + n)

    output(turns - 1)

    for o in range(1, n_seq):
        @pl.loop(0, 3 * parts)
        def _(n):
            share(o, n).wait_send()

    for i in range(TURNS):
        @pl.when(d < n_dp - 1)
        def _():
            first(i, True).wait_send()

        @pl.when(d > 0)
        def _():
            first(i, False).wait_send()

    @pl.loop(0, turns)
    def _(t):
        i = t % TURNS

        def one(s, up):
            @pl.when(d < n_dp - 1 if up else d > 0)
            def _():
                along(s, i, up).wait_send()

            to_x(s, i, z_block(i)).wait_send()
            to_y(s, i, z_block(i)).wait_send()

        for_sources(t // TURNS + 1, one)

    @pl.loop(0, n_dp)
    def _(s):
        @pl.loop(1, n_seq - c)
        def _(o):
            state_to(s, o).wait_send()

        @pl.when(s != d)
        def _():
            to_owner(s).wait_send()
            at = pl.ds(pl.multiple_of(s * cols, cols), cols)
            remote(stage.at[s], out.at[0, :, at], o_send.at[s], o_recv.at[s], dp=s).wait_recv()

    keep(d).wait()


def body(sizes, tokens, proj_weights, norm_gain):
    n_seq, n_heads, n_dp = sizes
    _, length, width = tokens.shape
    _, rows, cols = proj_weights.shape
    pieces = n_heads * SUBS
    block = width // pieces
    heads = cols // DH
    copies = 3 * (rows // min(rows, block))
    dma = pltpu.SemaphoreType.DMA
    hbm = pl.BlockSpec(memory_space=pltpu.HBM)
    flops = 2 * n_dp * length * width * 3 * cols
    return pl.pallas_call(
        functools.partial(kernel, sizes),
        out_shape=jax.ShapeDtypeStruct((1, length, n_dp * cols), jnp.bfloat16),
        in_specs=[hbm, hbm, pl.BlockSpec(memory_space=pltpu.VMEM)],
        out_specs=hbm,
        scratch_shapes=[
            pltpu.VMEM((n_dp, pieces, length, block), jnp.bfloat16),
            pltpu.VMEM((length, width), jnp.bfloat16),
            pltpu.VMEM((3, width, cols), jnp.bfloat16),
            pltpu.VMEM((n_dp, 3, length, cols), jnp.float32),
            pltpu.VMEM((n_dp, length, cols), jnp.bfloat16),
            pltpu.VMEM((n_dp, length, cols), jnp.bfloat16),
            pltpu.VMEM((n_dp, length, cols), jnp.bfloat16),
            pltpu.VMEM((n_dp, length, cols), jnp.bfloat16),
            pltpu.VMEM((n_dp, heads, DH, DH), jnp.bfloat16),
            pltpu.VMEM((n_seq - 1, n_dp, heads, DH, DH), jnp.bfloat16),
            dma, dma, dma((n_seq - 1, copies)), dma((n_seq - 1, copies)),
            dma((n_dp, TURNS)), dma((n_dp, TURNS)), dma((n_dp, TURNS)),
            dma((n_dp, TURNS)), dma((n_dp, TURNS)), dma((n_dp, TURNS)), dma((n_dp, TURNS)),
            dma((n_seq - 1, n_dp)), dma((n_seq - 1, n_dp)),
            dma((n_dp,)), dma((n_dp,)), dma,
        ],
        compiler_params=pltpu.CompilerParams(
            collective_id=0, has_side_effects=True, vmem_limit_bytes=(64 * 1024 - 512) * 1024
        ),
        cost_estimate=pl.CostEstimate(
            flops=flops, bytes_accessed=2 * (tokens.size + proj_weights.size), transcendentals=0
        ),
    )(tokens, proj_weights, norm_gain.reshape(1, cols))


def solution(mesh):
    sizes = tuple(mesh.shape[name] for name in ("seq", "heads", "dp"))
    in_specs = (P("dp", "seq", None), P(None, "seq", ("heads", "dp")), P(("heads", "dp")))
    out_specs = P("dp", "seq", "heads")
    return jax.shard_map(
        functools.partial(body, sizes), mesh=mesh, in_specs=in_specs, out_specs=out_specs, check_vma=False
    )
```

```python
import functools

import jax
import jax.numpy as jnp
from jax import lax
from jax.experimental import pallas as pl
from jax.experimental.pallas import tpu as pltpu
from jax.sharding import PartitionSpec as P

DH = 128
SUBS = 3
TURNS = SUBS + 1
LAG = 2
START = 5
EVEN = 2 * START - LAG
OWN_AT = 2
MESH = pl.DeviceIdType.MESH


def kernel(
    sizes, tokens, weights, gain, out,
    tok, own, w, acc, queries, keys, values, stage, state_out, state_in,
    own_sem, w_sem, w_send, w_recv, up_send, down_send, z_recv,
    x_send, x_recv, y_send, y_recv, st_send, st_recv, o_send, o_recv, o_sem,
):
    n_seq, n_heads, n_dp = sizes
    c, h, d = lax.axis_index("seq"), lax.axis_index("heads"), lax.axis_index("dp")
    length = own.shape[0]
    rows, cols = weights.shape[1], weights.shape[2]
    block = tok.shape[3]
    heads = cols // DH
    xp = h + 1 - 2 * (h % 2)
    yp = h + 2 - 4 * (h // 2)
    across = xp + yp - h

    def remote(src, dst, send, recv, **device):
        return pltpu.make_async_remote_copy(
            src_ref=src, dst_ref=dst, send_sem=send, recv_sem=recv,
            device_id=device, device_id_type=MESH,
        )

    own_copy = pltpu.make_async_copy(tokens.at[0], own, own_sem)
    own_copy.start()
    my_rows = w.at[:, pl.ds(pl.multiple_of(c * rows, 16), rows), :]
    w_copy = pltpu.make_async_copy(weights, my_rows, w_sem)
    w_copy.start()

    barrier = pltpu.get_barrier_semaphore()
    for o in range(1, n_dp):
        pl.semaphore_signal(barrier, inc=1, device_id={"dp": (d + o) % n_dp}, device_id_type=MESH)
    for o in range(1, n_seq):
        pl.semaphore_signal(barrier, inc=1, device_id={"seq": (c + o) % n_seq}, device_id_type=MESH)
    pl.semaphore_signal(barrier, inc=1, device_id={"heads": xp}, device_id_type=MESH)
    pl.semaphore_signal(barrier, inc=1, device_id={"heads": yp}, device_id_type=MESH)
    pl.semaphore_wait(barrier, n_dp + n_seq)

    def z_block(i):
        last = i // SUBS
        return (1 - last) * (h * SUBS + SUBS - 1 - i) + last * across * SUBS

    def x_block(i):
        last = i // SUBS
        return (1 - last) * (xp * SUBS + SUBS - 1 - i) + last * (across * SUBS + 1)

    def y_block(i):
        last = i // SUBS
        return (1 - last) * (yp * SUBS + SUBS - 1 - i) + last * (across * SUBS + 2)

    def first(i, up):
        b = z_block(i)
        src = tokens.at[0, :, pl.ds(pl.multiple_of(b * block, block), block)]
        return remote(
            src, tok.at[d, b], (up_send if up else down_send).at[d, i], z_recv.at[d, i],
            dp=d + 1 if up else d - 1,
        )

    def along(s, i, up):
        b = z_block(i)
        return remote(
            tok.at[s, b], tok.at[s, b], (up_send if up else down_send).at[s, i],
            z_recv.at[s, i], dp=d + 1 if up else d - 1,
        )

    def to_x(s, i, b):
        return remote(tok.at[s, b], tok.at[s, b], x_send.at[s, i], x_recv.at[s, i], heads=xp)

    def to_y(s, i, b):
        return remote(tok.at[s, b], tok.at[s, b], y_send.at[s, i], y_recv.at[s, i], heads=yp)

    for i in range(TURNS):
        @pl.when(d < n_dp - 1)
        def _():
            first(i, True).start()

        @pl.when(d > 0)
        def _():
            first(i, False).start()

    def share(o, j):
        return remote(
            my_rows.at[j], my_rows.at[j], w_send.at[o - 1, j], w_recv.at[o - 1, j],
            seq=(c + o) % n_seq,
        )

    acc[...] = jnp.zeros_like(acc)
    w_copy.wait()
    for o in range(1, n_seq):
        for j in range(3):
            share(o, j).start()

    def for_sources(k, do):
        @pl.when(d - k >= 0)
        def _():
            do(d - k, True)

        @pl.when(d + k < n_dp)
        def _():
            do(d + k, False)

    def z_phase(t):
        i = t % TURNS

        def one(s, up):
            b = z_block(i)
            along(s, i, up).wait_recv()
            @pl.when(d < n_dp - 1 if up else d > 0)
            def _():
                along(s, i, up).start()

            @pl.when(i < SUBS)
            def _():
                to_x(s, i, b).start()
                to_y(s, i, b).start()

        for_sources(t // TURNS + 1, one)

    def xy_phase(t):
        i = t % TURNS

        def one(s, up):
            to_x(s, i, x_block(i)).wait_recv()

            @pl.when(i == 0)
            def _():
                to_y(s, SUBS, x_block(0)).start()

            to_y(s, i, y_block(i)).wait_recv()

            @pl.when(i == 1)
            def _():
                to_x(s, SUBS, y_block(1)).start()

        for_sources(t // TURNS + 1, one)

    def rows_of(s, blocks):
        return jnp.concatenate([tok[s, b] for b in blocks], axis=1)

    def own_rows(blocks):
        return jnp.concatenate(
            [own[:, pl.ds(pl.multiple_of(b * block, block), block)] for b in blocks], axis=1
        )

    def multiply(i, blocks, parts):
        piece = jnp.concatenate([rows for _, rows in parts], axis=0)

        def add(j):
            k_rows = [pl.ds(pl.multiple_of(b * block, block), block) for b in blocks]
            weight = jnp.concatenate([w[j, at, :] for at in k_rows], axis=0)
            product = jnp.dot(piece, weight, preferred_element_type=jnp.float32)
            for n, (s, _) in enumerate(parts):
                acc[s, j] += product[n * length:(n + 1) * length]

        add(1)
        add(2)

        @pl.when(i == TURNS - 1)
        def _():
            for s, _ in parts:
                make_state(s)

        add(0)

        @pl.when(i == TURNS - 1)
        def _():
            for s, _ in parts:
                finish_local(s)

    def state_to(s, o):
        return remote(
            state_out.at[s], state_in.at[o - 1, s], st_send.at[o - 1, s], st_recv.at[o - 1, s],
            seq=(c + o) % n_seq,
        )

    def silu(v):
        return v / (1.0 + jnp.exp(-v))

    def make_state(s):
        for head in range(heads):
            at = slice(head * DH, (head + 1) * DH)
            k = silu(acc[s, 1, :, at]).astype(jnp.bfloat16)
            v = acc[s, 2, :, at].astype(jnp.bfloat16)
            state = lax.dot_general(k, v, (((0,), (0,)), ((), ())), preferred_element_type=jnp.float32)
            state_out[s, head] = state.astype(jnp.bfloat16)
            keys[s, :, at] = k
            values[s, :, at] = v

        @pl.loop(1, n_seq - c)
        def _(o):
            state_to(s, o).start()

    def finish_local(s):
        causal = lax.broadcasted_iota(jnp.int32, (length, length), 0) >= lax.broadcasted_iota(
            jnp.int32, (length, length), 1
        )
        for head in range(heads):
            at = slice(head * DH, (head + 1) * DH)
            q = silu(acc[s, 0, :, at]).astype(jnp.bfloat16)
            scores = lax.dot_general(
                q, keys[s, :, at], (((1,), (1,)), ((), ())), preferred_element_type=jnp.float32
            )
            scores_b = jnp.where(causal, scores, 0.0).astype(jnp.bfloat16)
            queries[s, :, at] = q
            acc[s, 0, :, at] = jnp.dot(
                scores_b, values[s, :, at], preferred_element_type=jnp.float32
            )

    def to_owner(s):
        at = pl.ds(pl.multiple_of(d * cols, cols), cols)
        return remote(stage.at[s], out.at[0, :, at], o_send.at[s], o_recv.at[d], dp=s)

    def keep(s):
        at = pl.ds(pl.multiple_of(d * cols, cols), cols)
        return pltpu.make_async_copy(stage.at[s], out.at[0, :, at], o_sem)

    def finish_carried(s):
        @pl.when(c > 0)
        def _():
            @pl.loop(1, c + 1)
            def _(o):
                state_to(s, o).wait_recv()

            for head in range(heads):
                at = slice(head * DH, (head + 1) * DH)
                prefix = lax.fori_loop(
                    1, c + 1,
                    lambda o, total: total + state_in[o - 1, s, head].astype(jnp.float32),
                    jnp.zeros((DH, DH), jnp.float32),
                )
                acc[s, 0, :, at] += jnp.dot(
                    queries[s, :, at], prefix.astype(jnp.bfloat16),
                    preferred_element_type=jnp.float32,
                )

        for head in range(heads):
            at = slice(head * DH, (head + 1) * DH)
            attn = acc[s, 0, :, at]
            scale = lax.rsqrt(jnp.mean(attn * attn, axis=-1, keepdims=True) + 1e-06)
            stage[s, :, at] = (attn * scale * gain[:, at]).astype(jnp.bfloat16)

    def compute(t):
        i = t % TURNS
        k = t // TURNS + 1
        blocks = (z_block(i), x_block(i), y_block(i))
        below = (d + n_dp - k) // n_dp
        above = (2 * n_dp - 1 - d - k) // n_dp

        @pl.when(below + above == 2)
        def _():
            multiply(i, blocks, [(s, rows_of(s, blocks)) for s in (d - k, d + k)])

        @pl.when(below + above == 1)
        def _():
            s = d + k - 2 * k * below

            @pl.when(k == OWN_AT)
            def _():
                multiply(i, blocks, [(d, own_rows(blocks)), (s, rows_of(s, blocks))])

            @pl.when(k != OWN_AT)
            def _():
                multiply(i, blocks, [(s, rows_of(s, blocks))])

        if 2 * OWN_AT < n_dp:
            @pl.when((k == OWN_AT) & (below + above != 1))
            def _():
                multiply(i, blocks, [(d, own_rows(blocks))])

    def output(t):
        @pl.when(t % TURNS == TURNS - 1)
        def _():
            @pl.when(t // TURNS + 1 == OWN_AT)
            def _():
                finish_carried(d)
                keep(d).start()

            def one(s, up):
                finish_carried(s)
                to_owner(s).start()

            for_sources(t // TURNS + 1, one)

    turns = (n_dp - 1) * TURNS
    for t in range(START):
        z_phase(t)
        if t >= LAG:
            xy_phase(t - LAG)
    own_copy.wait()
    for o in range(1, n_seq):
        for j in range(3):
            share(o, j).wait_recv()

    @pl.loop(START, EVEN)
    def _(t):
        z_phase(t)
        xy_phase(t - LAG)

        @pl.loop(0, 2)
        def _(n):
            @pl.when(t > START)
            def _():
                output(2 * (t - 1 - START) + n)

            compute(2 * (t - START) + n)

    late = turns - TURNS

    @pl.loop(EVEN, late + 1)
    def _(t):
        z_phase(t)
        xy_phase(t - LAG)
        output(t - LAG - 1)
        compute(t - LAG)

    xy_phase(late - 1)
    compute(late - 1)

    @pl.loop(late + 1, turns + 1)
    def _(t):
        @pl.when(t < turns)
        def _():
            z_phase(t)

        xy_phase(t - 1)
        output(t - 2)
        compute(t - 1)

    output(turns - 1)

    for o in range(1, n_seq):
        for j in range(3):
            share(o, j).wait_send()

    for i in range(TURNS):
        @pl.when(d < n_dp - 1)
        def _():
            first(i, True).wait_send()

        @pl.when(d > 0)
        def _():
            first(i, False).wait_send()

    @pl.loop(0, turns)
    def _(t):
        i = t % TURNS

        def one(s, up):
            @pl.when(d < n_dp - 1 if up else d > 0)
            def _():
                along(s, i, up).wait_send()

            to_x(s, i, z_block(i)).wait_send()
            to_y(s, i, z_block(i)).wait_send()

        for_sources(t // TURNS + 1, one)

    @pl.loop(0, n_dp)
    def _(s):
        @pl.loop(1, n_seq - c)
        def _(o):
            state_to(s, o).wait_send()

        @pl.when(s != d)
        def _():
            to_owner(s).wait_send()
            at = pl.ds(pl.multiple_of(s * cols, cols), cols)
            remote(stage.at[s], out.at[0, :, at], o_send.at[s], o_recv.at[s], dp=s).wait_recv()

    keep(d).wait()


def body(sizes, tokens, proj_weights, norm_gain):
    n_seq, n_heads, n_dp = sizes
    _, length, width = tokens.shape
    _, rows, cols = proj_weights.shape
    pieces = n_heads * SUBS
    block = width // pieces
    heads = cols // DH
    dma = pltpu.SemaphoreType.DMA
    hbm = pl.BlockSpec(memory_space=pltpu.HBM)
    flops = 2 * n_dp * length * width * 3 * cols
    return pl.pallas_call(
        functools.partial(kernel, sizes),
        out_shape=jax.ShapeDtypeStruct((1, length, n_dp * cols), jnp.bfloat16),
        in_specs=[hbm, hbm, pl.BlockSpec(memory_space=pltpu.VMEM)],
        out_specs=hbm,
        scratch_shapes=[
            pltpu.VMEM((n_dp, pieces, length, block), jnp.bfloat16),
            pltpu.VMEM((length, width), jnp.bfloat16),
            pltpu.VMEM((3, width, cols), jnp.bfloat16),
            pltpu.VMEM((n_dp, 3, length, cols), jnp.float32),
            pltpu.VMEM((n_dp, length, cols), jnp.bfloat16),
            pltpu.VMEM((n_dp, length, cols), jnp.bfloat16),
            pltpu.VMEM((n_dp, length, cols), jnp.bfloat16),
            pltpu.VMEM((n_dp, length, cols), jnp.bfloat16),
            pltpu.VMEM((n_dp, heads, DH, DH), jnp.bfloat16),
            pltpu.VMEM((n_seq - 1, n_dp, heads, DH, DH), jnp.bfloat16),
            dma, dma, dma((n_seq - 1, 3)), dma((n_seq - 1, 3)),
            dma((n_dp, TURNS)), dma((n_dp, TURNS)), dma((n_dp, TURNS)),
            dma((n_dp, TURNS)), dma((n_dp, TURNS)), dma((n_dp, TURNS)), dma((n_dp, TURNS)),
            dma((n_seq - 1, n_dp)), dma((n_seq - 1, n_dp)),
            dma((n_dp,)), dma((n_dp,)), dma,
        ],
        compiler_params=pltpu.CompilerParams(
            collective_id=0, has_side_effects=True, vmem_limit_bytes=(64 * 1024 - 11008) * 1024
        ),
        cost_estimate=pl.CostEstimate(
            flops=flops, bytes_accessed=2 * (tokens.size + proj_weights.size), transcendentals=0
        ),
    )(tokens, proj_weights, norm_gain.reshape(1, cols))


def solution(mesh):
    sizes = tuple(mesh.shape[name] for name in ("seq", "heads", "dp"))
    in_specs = (P("dp", "seq", None), P(None, "seq", ("heads", "dp")), P(("heads", "dp")))
    out_specs = P("dp", "seq", "heads")
    return jax.shard_map(
        functools.partial(body, sizes), mesh=mesh, in_specs=in_specs, out_specs=out_specs, check_vma=False
    )
```

```python
import functools

import jax
import jax.numpy as jnp
from jax import lax
from jax.experimental import pallas as pl
from jax.experimental.pallas import tpu as pltpu
from jax.sharding import PartitionSpec as P

DH = 128
SUBS = 3
TURNS = SUBS + 1
LAG = 2
START = 4
EVEN = 2 * START - LAG
OWN_AT = 2
MESH = pl.DeviceIdType.MESH


def kernel(
    sizes, tokens, weights, gain, out,
    tok, own, w, acc, queries, keys, values, stage, state_out, state_in,
    own_sem, w_sem, w_send, w_recv, up_send, down_send, z_recv,
    x_send, x_recv, y_send, y_recv, st_send, st_recv, o_send, o_recv, o_sem,
):
    n_seq, n_heads, n_dp = sizes
    c, h, d = lax.axis_index("seq"), lax.axis_index("heads"), lax.axis_index("dp")
    length = own.shape[0]
    rows, cols = weights.shape[1], weights.shape[2]
    block = tok.shape[3]
    heads = cols // DH
    xp = h + 1 - 2 * (h % 2)
    yp = h + 2 - 4 * (h // 2)
    across = xp + yp - h

    def remote(src, dst, send, recv, **device):
        return pltpu.make_async_remote_copy(
            src_ref=src, dst_ref=dst, send_sem=send, recv_sem=recv,
            device_id=device, device_id_type=MESH,
        )

    own_copy = pltpu.make_async_copy(tokens.at[0], own, own_sem)
    own_copy.start()
    my_rows = w.at[:, pl.ds(pl.multiple_of(c * rows, 16), rows), :]
    w_copy = pltpu.make_async_copy(weights, my_rows, w_sem)
    w_copy.start()

    barrier = pltpu.get_barrier_semaphore()
    for o in range(1, n_dp):
        pl.semaphore_signal(barrier, inc=1, device_id={"dp": (d + o) % n_dp}, device_id_type=MESH)
    for o in range(1, n_seq):
        pl.semaphore_signal(barrier, inc=1, device_id={"seq": (c + o) % n_seq}, device_id_type=MESH)
    pl.semaphore_signal(barrier, inc=1, device_id={"heads": xp}, device_id_type=MESH)
    pl.semaphore_signal(barrier, inc=1, device_id={"heads": yp}, device_id_type=MESH)
    pl.semaphore_wait(barrier, n_dp + n_seq)

    def z_block(i):
        last = i // SUBS
        return (1 - last) * (h * SUBS + SUBS - 1 - i) + last * across * SUBS

    def x_block(i):
        last = i // SUBS
        return (1 - last) * (xp * SUBS + SUBS - 1 - i) + last * (across * SUBS + 1)

    def y_block(i):
        last = i // SUBS
        return (1 - last) * (yp * SUBS + SUBS - 1 - i) + last * (across * SUBS + 2)

    def first(i, up):
        b = z_block(i)
        src = tokens.at[0, :, pl.ds(pl.multiple_of(b * block, block), block)]
        return remote(
            src, tok.at[d, b], (up_send if up else down_send).at[d, i], z_recv.at[d, i],
            dp=d + 1 if up else d - 1,
        )

    def along(s, i, up):
        b = z_block(i)
        return remote(
            tok.at[s, b], tok.at[s, b], (up_send if up else down_send).at[s, i],
            z_recv.at[s, i], dp=d + 1 if up else d - 1,
        )

    def to_x(s, i, b):
        return remote(tok.at[s, b], tok.at[s, b], x_send.at[s, i], x_recv.at[s, i], heads=xp)

    def to_y(s, i, b):
        return remote(tok.at[s, b], tok.at[s, b], y_send.at[s, i], y_recv.at[s, i], heads=yp)

    for i in range(TURNS):
        @pl.when(d < n_dp - 1)
        def _():
            first(i, True).start()

        @pl.when(d > 0)
        def _():
            first(i, False).start()

    def share(o, j):
        return remote(
            my_rows.at[j], my_rows.at[j], w_send.at[o - 1, j], w_recv.at[o - 1, j],
            seq=(c + o) % n_seq,
        )

    acc[...] = jnp.zeros_like(acc)
    w_copy.wait()
    for o in range(1, n_seq):
        for j in range(3):
            share(o, j).start()

    def for_sources(k, do):
        @pl.when(d - k >= 0)
        def _():
            do(d - k, True)

        @pl.when(d + k < n_dp)
        def _():
            do(d + k, False)

    def z_phase(t):
        i = t % TURNS

        def one(s, up):
            b = z_block(i)
            along(s, i, up).wait_recv()
            @pl.when(d < n_dp - 1 if up else d > 0)
            def _():
                along(s, i, up).start()

            @pl.when(i < SUBS)
            def _():
                to_x(s, i, b).start()
                to_y(s, i, b).start()

        for_sources(t // TURNS + 1, one)

    def xy_phase(t):
        i = t % TURNS

        def one(s, up):
            to_x(s, i, x_block(i)).wait_recv()

            @pl.when(i == 0)
            def _():
                to_y(s, SUBS, x_block(0)).start()

            to_y(s, i, y_block(i)).wait_recv()

            @pl.when(i == 1)
            def _():
                to_x(s, SUBS, y_block(1)).start()

        for_sources(t // TURNS + 1, one)

    def rows_of(s, blocks):
        return jnp.concatenate([tok[s, b] for b in blocks], axis=1)

    def own_rows(blocks):
        return jnp.concatenate(
            [own[:, pl.ds(pl.multiple_of(b * block, block), block)] for b in blocks], axis=1
        )

    def multiply(i, blocks, parts):
        piece = jnp.concatenate([rows for _, rows in parts], axis=0)

        def add(j):
            k_rows = [pl.ds(pl.multiple_of(b * block, block), block) for b in blocks]
            weight = jnp.concatenate([w[j, at, :] for at in k_rows], axis=0)
            product = jnp.dot(piece, weight, preferred_element_type=jnp.float32)
            for n, (s, _) in enumerate(parts):
                acc[s, j] += product[n * length:(n + 1) * length]

        add(1)
        add(2)

        @pl.when(i == TURNS - 1)
        def _():
            for s, _ in parts:
                make_state(s)

        add(0)

        @pl.when(i == TURNS - 1)
        def _():
            for s, _ in parts:
                finish_local(s)

    def state_to(s, o):
        return remote(
            state_out.at[s], state_in.at[o - 1, s], st_send.at[o - 1, s], st_recv.at[o - 1, s],
            seq=(c + o) % n_seq,
        )

    def silu(v):
        return v / (1.0 + jnp.exp(-v))

    def make_state(s):
        for head in range(heads):
            at = slice(head * DH, (head + 1) * DH)
            k = silu(acc[s, 1, :, at]).astype(jnp.bfloat16)
            v = acc[s, 2, :, at].astype(jnp.bfloat16)
            state = lax.dot_general(k, v, (((0,), (0,)), ((), ())), preferred_element_type=jnp.float32)
            state_out[s, head] = state.astype(jnp.bfloat16)
            keys[s, :, at] = k
            values[s, :, at] = v

        @pl.loop(1, n_seq - c)
        def _(o):
            state_to(s, o).start()

    def finish_local(s):
        causal = lax.broadcasted_iota(jnp.int32, (length, length), 0) >= lax.broadcasted_iota(
            jnp.int32, (length, length), 1
        )
        for head in range(heads):
            at = slice(head * DH, (head + 1) * DH)
            q = silu(acc[s, 0, :, at]).astype(jnp.bfloat16)
            scores = lax.dot_general(
                q, keys[s, :, at], (((1,), (1,)), ((), ())), preferred_element_type=jnp.float32
            )
            scores_b = jnp.where(causal, scores, 0.0).astype(jnp.bfloat16)
            queries[s, :, at] = q
            acc[s, 0, :, at] = jnp.dot(
                scores_b, values[s, :, at], preferred_element_type=jnp.float32
            )

    def to_owner(s):
        at = pl.ds(pl.multiple_of(d * cols, cols), cols)
        return remote(stage.at[s], out.at[0, :, at], o_send.at[s], o_recv.at[d], dp=s)

    def keep(s):
        at = pl.ds(pl.multiple_of(d * cols, cols), cols)
        return pltpu.make_async_copy(stage.at[s], out.at[0, :, at], o_sem)

    def finish_carried(s):
        @pl.when(c > 0)
        def _():
            @pl.loop(1, c + 1)
            def _(o):
                state_to(s, o).wait_recv()

            for head in range(heads):
                at = slice(head * DH, (head + 1) * DH)
                prefix = lax.fori_loop(
                    1, c + 1,
                    lambda o, total: total + state_in[o - 1, s, head].astype(jnp.float32),
                    jnp.zeros((DH, DH), jnp.float32),
                )
                acc[s, 0, :, at] += jnp.dot(
                    queries[s, :, at], prefix.astype(jnp.bfloat16),
                    preferred_element_type=jnp.float32,
                )

        for head in range(heads):
            at = slice(head * DH, (head + 1) * DH)
            attn = acc[s, 0, :, at]
            scale = lax.rsqrt(jnp.mean(attn * attn, axis=-1, keepdims=True) + 1e-06)
            stage[s, :, at] = (attn * scale * gain[:, at]).astype(jnp.bfloat16)

    def compute(t):
        i = t % TURNS
        k = t // TURNS + 1
        blocks = (z_block(i), x_block(i), y_block(i))
        below = (d + n_dp - k) // n_dp
        above = (2 * n_dp - 1 - d - k) // n_dp

        @pl.when(below + above == 2)
        def _():
            multiply(i, blocks, [(s, rows_of(s, blocks)) for s in (d - k, d + k)])

        @pl.when(below + above == 1)
        def _():
            s = d + k - 2 * k * below

            @pl.when(k == OWN_AT)
            def _():
                multiply(i, blocks, [(d, own_rows(blocks)), (s, rows_of(s, blocks))])

            @pl.when(k != OWN_AT)
            def _():
                multiply(i, blocks, [(s, rows_of(s, blocks))])

        if 2 * OWN_AT < n_dp:
            @pl.when((k == OWN_AT) & (below + above != 1))
            def _():
                multiply(i, blocks, [(d, own_rows(blocks))])

    def output(t):
        @pl.when(t % TURNS == TURNS - 1)
        def _():
            @pl.when(t // TURNS + 1 == OWN_AT)
            def _():
                finish_carried(d)
                keep(d).start()

            def one(s, up):
                finish_carried(s)
                to_owner(s).start()

            for_sources(t // TURNS + 1, one)

    turns = (n_dp - 1) * TURNS
    for t in range(START):
        z_phase(t)
        if t >= LAG:
            xy_phase(t - LAG)
    own_copy.wait()
    for o in range(1, n_seq):
        for j in range(3):
            share(o, j).wait_recv()

    @pl.loop(START, EVEN)
    def _(t):
        z_phase(t)
        xy_phase(t - LAG)

        @pl.loop(0, 2)
        def _(n):
            @pl.when(t > START)
            def _():
                output(2 * (t - 1 - START) + n)

            compute(2 * (t - START) + n)

    late = turns - TURNS

    @pl.loop(EVEN, late + 1)
    def _(t):
        z_phase(t)
        xy_phase(t - LAG)
        output(t - LAG - 1)
        compute(t - LAG)

    xy_phase(late - 1)
    compute(late - 1)

    @pl.loop(late + 1, turns + 1)
    def _(t):
        @pl.when(t < turns)
        def _():
            z_phase(t)

        xy_phase(t - 1)
        output(t - 2)
        compute(t - 1)

    output(turns - 1)

    for o in range(1, n_seq):
        for j in range(3):
            share(o, j).wait_send()

    for i in range(TURNS):
        @pl.when(d < n_dp - 1)
        def _():
            first(i, True).wait_send()

        @pl.when(d > 0)
        def _():
            first(i, False).wait_send()

    @pl.loop(0, turns)
    def _(t):
        i = t % TURNS

        def one(s, up):
            @pl.when(d < n_dp - 1 if up else d > 0)
            def _():
                along(s, i, up).wait_send()

            to_x(s, i, z_block(i)).wait_send()
            to_y(s, i, z_block(i)).wait_send()

        for_sources(t // TURNS + 1, one)

    @pl.loop(0, n_dp)
    def _(s):
        @pl.loop(1, n_seq - c)
        def _(o):
            state_to(s, o).wait_send()

        @pl.when(s != d)
        def _():
            to_owner(s).wait_send()
            at = pl.ds(pl.multiple_of(s * cols, cols), cols)
            remote(stage.at[s], out.at[0, :, at], o_send.at[s], o_recv.at[s], dp=s).wait_recv()

    keep(d).wait()


def body(sizes, tokens, proj_weights, norm_gain):
    n_seq, n_heads, n_dp = sizes
    _, length, width = tokens.shape
    _, rows, cols = proj_weights.shape
    pieces = n_heads * SUBS
    block = width // pieces
    heads = cols // DH
    dma = pltpu.SemaphoreType.DMA
    hbm = pl.BlockSpec(memory_space=pltpu.HBM)
    flops = 2 * n_dp * length * width * 3 * cols
    return pl.pallas_call(
        functools.partial(kernel, sizes),
        out_shape=jax.ShapeDtypeStruct((1, length, n_dp * cols), jnp.bfloat16),
        in_specs=[hbm, hbm, pl.BlockSpec(memory_space=pltpu.VMEM)],
        out_specs=hbm,
        scratch_shapes=[
            pltpu.VMEM((n_dp, pieces, length, block), jnp.bfloat16),
            pltpu.VMEM((length, width), jnp.bfloat16),
            pltpu.VMEM((3, width, cols), jnp.bfloat16),
            pltpu.VMEM((n_dp, 3, length, cols), jnp.float32),
            pltpu.VMEM((n_dp, length, cols), jnp.bfloat16),
            pltpu.VMEM((n_dp, length, cols), jnp.bfloat16),
            pltpu.VMEM((n_dp, length, cols), jnp.bfloat16),
            pltpu.VMEM((n_dp, length, cols), jnp.bfloat16),
            pltpu.VMEM((n_dp, heads, DH, DH), jnp.bfloat16),
            pltpu.VMEM((n_seq - 1, n_dp, heads, DH, DH), jnp.bfloat16),
            dma, dma, dma((n_seq - 1, 3)), dma((n_seq - 1, 3)),
            dma((n_dp, TURNS)), dma((n_dp, TURNS)), dma((n_dp, TURNS)),
            dma((n_dp, TURNS)), dma((n_dp, TURNS)), dma((n_dp, TURNS)), dma((n_dp, TURNS)),
            dma((n_seq - 1, n_dp)), dma((n_seq - 1, n_dp)),
            dma((n_dp,)), dma((n_dp,)), dma,
        ],
        compiler_params=pltpu.CompilerParams(
            collective_id=0, has_side_effects=True, vmem_limit_bytes=(64 * 1024 - 11008) * 1024
        ),
        cost_estimate=pl.CostEstimate(
            flops=flops, bytes_accessed=2 * (tokens.size + proj_weights.size), transcendentals=0
        ),
    )(tokens, proj_weights, norm_gain.reshape(1, cols))


def solution(mesh):
    sizes = tuple(mesh.shape[name] for name in ("seq", "heads", "dp"))
    in_specs = (P("dp", "seq", None), P(None, "seq", ("heads", "dp")), P(("heads", "dp")))
    out_specs = P("dp", "seq", "heads")
    return jax.shard_map(
        functools.partial(body, sizes), mesh=mesh, in_specs=in_specs, out_specs=out_specs, check_vma=False
    )
```
